512 devices in a mesh: pipe: 4 (over z_lo), lon: 32 (over x, y), lat: 4 (over z_hi, core).
Axes of the slice: x: 4, y: 8, z: 8 (z_hi: 2, z_lo: 4; z = z_hi * 4 + z_lo), core: 2. Of those that a mesh axis runs over, the one named last changes fastest.
Arguments:
- acts: bfloat16 [4, 2, 24, 768, 512], P('pipe', None, 'lat', 'lon'), may hold values from -6 to 6
- section_grads: bfloat16 [4, 2, 24, 768, 512], P('pipe', None, 'lat', 'lon'), may hold values from -6 to 6
- gain: float32 [4, 512], P('pipe'), may hold values from 0.1 to 1.9
- w_qkv: bfloat16 [4, 512, 1536], P('pipe'), may hold values from -0.25 to 0.25
- w_out: bfloat16 [4, 512, 512], P('pipe'), may hold values from -0.25 to 0.25
- labels: int32 [24, 768], replicated, may hold values from 0 to 7, as said below
Outputs:
- grad_input: bfloat16 [4, 2, 24, 768, 512], P('pipe', None, 'lat', 'lon')
- grad_wo: float32 [2048, 512], P(('pipe', 'lon', 'lat'))
The draws below stay inside these ranges and needn't reach their ends.
Inputs may be any that keep to these rules, and one draw needn't show every extreme that they name: `labels`: A cell's label is b + 2 r: b is 1 on the first latitude rows of the initial grid (1 to 3 rows, drawn for each longitude), else 0; r is a region number of 0 to 3 drawn for each cell. A token attends to the tokens of its window that carry the same label.
All inputs are finite; a program needn't handle non-finite values.
Results may differ from the reference program's by a relative error of at most 0.0095.
Values may be sent and summed in bfloat16 or wider, within the bound.
A program may use at most 64 MiB of HBM per device.

```python
import jax
import jax.numpy as jnp
from jax import lax

D = 512
HEAD_DIM = 64
LEV = 2
WIN_LAT = 6
WIN_LON = 12
SHIFT_LAT = 3
SHIFT_LON = 6
NLAT = 24
NLON = 768
SECTIONS = 4


def draw_labels(key, part):
    key = jax.random.fold_in(key, 7)
    band_key, region_key = jax.random.split(key)
    band_rows = jax.random.randint(band_key, (NLON,), 1, SHIFT_LAT + 1)
    row_ids = jnp.arange(NLAT, dtype=jnp.int32)[:, None]
    band = (row_ids < band_rows[None, :]).astype(jnp.int32)
    region = jax.random.randint(region_key, (NLAT, NLON), 0, 4).astype(jnp.int32)
    region = region.at[0, 0].set(3).at[NLAT - 1, 0].set(0)
    return (band + 2 * region).astype(jnp.int32)


def shard_levels(stream_key, extent, cuts, smallest, largest):
    def one(axis_at, blocks):
        draws = jax.random.uniform(jax.random.fold_in(jax.random.fold_in(stream_key, 6), axis_at), (blocks,), jnp.float32, smallest / len(cuts), largest / len(cuts))
        return jnp.repeat(jnp.exp(draws), extent[axis_at] // blocks).reshape((-1,) + (1,) * (len(extent) - axis_at - 1))

    level = one(*cuts[0])
    for cut in cuts[1:]:
        level = level * one(*cut)
    return level


def bell_draw(own_key, shape, spread, bound, cuts=(), kind=jnp.bfloat16):
    drawn = jax.random.normal(own_key, shape, jnp.float32) * spread
    if len(cuts) > 0:
        drawn = shard_levels(own_key, shape, cuts, -0.22, 0.18) * drawn
    return jnp.clip(drawn, min=-bound, max=bound).astype(kind)


def setup_inputs(seed: int = 0) -> dict:
    streams_of = jax.random.split(jax.random.key(seed), 7)
    return {
        "acts": bell_draw(streams_of[0], (SECTIONS, LEV, NLAT, NLON, D), 1.0, 6.0, ((0, 4), (2, 4), (3, 32))),
        "section_grads": bell_draw(streams_of[1], (SECTIONS, LEV, NLAT, NLON, D), 1.0, 6.0, ((0, 4), (2, 4), (3, 32))),
        "gain": jnp.clip(1.0 + 0.18 * jax.random.normal(streams_of[2], (SECTIONS, D), jnp.float32), 0.1, 1.9),
        "w_qkv": bell_draw(streams_of[3], (SECTIONS, D, 3 * D), D ** -0.5, 0.25, ((0, 4),)),
        "w_out": bell_draw(streams_of[4], (SECTIONS, D, D), D ** -0.5, 0.25, ((0, 4),)),
        "labels": draw_labels(jax.random.fold_in(streams_of[6], 71), 0),
    }


epsilon = 1e-05
masked_score = -1e+30

def to_windows(layer_field):
    level_count, row_count, col_count, features = layer_field.shape
    lat_windows = row_count // WIN_LAT
    lon_windows = col_count // WIN_LON
    blocks = layer_field.reshape(level_count, lat_windows, WIN_LAT, lon_windows, WIN_LON, features)
    blocks = blocks.transpose(1, 3, 0, 2, 4, 5)
    return blocks.reshape(lat_windows * lon_windows, level_count * WIN_LAT * WIN_LON, features)

def from_windows(blocks, level_count, row_count, col_count):
    features = blocks.shape[-1]
    lat_windows = row_count // WIN_LAT
    lon_windows = col_count // WIN_LON
    layer_field = blocks.reshape(lat_windows, lon_windows, level_count, WIN_LAT, WIN_LON, features)
    return layer_field.transpose(2, 0, 3, 1, 4, 5).reshape(level_count, row_count, col_count, features)

def multiply(form, left, right):
    return jnp.einsum(form, left.astype(jnp.float32), right.astype(jnp.float32))

def normalize(layer_input, gain_row):
    values_f = layer_input.astype(jnp.float32)
    mean_value = lax.optimization_barrier(jnp.mean(values_f, -1, keepdims=True))
    variance = lax.optimization_barrier(jnp.mean((values_f - mean_value) ** 2, -1, keepdims=True))
    inverse = 1.0 / jnp.sqrt(variance + epsilon)
    centred = (values_f - mean_value) * inverse
    return ((centred * gain_row).astype(jnp.bfloat16), centred, inverse)

def attend_backward(projected, upstream, label_win, weight_out):
    window_count, token_count, triple = projected.shape
    width = triple // 3
    head_count = width // HEAD_DIM
    split_heads = projected.reshape(window_count, token_count, 3, head_count, HEAD_DIM)
    queries = split_heads[:, :, 0]
    key_rows = split_heads[:, :, 1]
    value_rows = split_heads[:, :, 2]
    score_scale = HEAD_DIM ** (-0.5)
    scores = multiply('wqhe,wkhe->whqk', queries, key_rows) * score_scale
    same_label = (label_win[:, :, None] == label_win[:, None, :])[:, None]
    scores = jnp.where(same_label, scores, masked_score)
    row_peak = lax.optimization_barrier(jnp.max(scores, -1, keepdims=True))
    exps = jnp.exp(scores - row_peak)
    weights = exps / lax.optimization_barrier(jnp.sum(exps, -1, keepdims=True))
    weights_low = weights.astype(jnp.bfloat16)
    attended = multiply('whqk,wkhe->wqhe', weights_low, value_rows).astype(jnp.bfloat16)
    attended = attended.reshape(window_count, token_count, width)
    grad_attended = multiply('wtd,ed->wte', upstream, weight_out).astype(jnp.bfloat16)
    grad_heads = grad_attended.reshape(window_count, token_count, head_count, HEAD_DIM)
    grad_weights = multiply('wqhe,wkhe->whqk', grad_heads, value_rows)
    inner = lax.optimization_barrier(jnp.sum(grad_weights * weights, -1, keepdims=True))
    grad_scores = (weights * (grad_weights - inner) * score_scale).astype(jnp.bfloat16)
    grad_query = multiply('whqk,wkhe->wqhe', grad_scores, key_rows)
    grad_keys = multiply('whqk,wqhe->wkhe', grad_scores, queries)
    grad_values = multiply('whqk,wqhe->wkhe', weights_low, grad_heads)
    grad_proj = jnp.stack([grad_query, grad_keys, grad_values], 2).astype(jnp.bfloat16)
    return (grad_proj.reshape(window_count, token_count, triple), attended)

def norm_backward(grad_proj, weight_in, gain_row, centred, inverse):
    width = weight_in.shape[0]
    lead = grad_proj.shape[:-1]
    grad_normed = jnp.dot(grad_proj.reshape(-1, 3 * width), weight_in.T, preferred_element_type=jnp.float32)
    scaled = grad_normed.reshape(lead + (width,)) * gain_row
    first = lax.optimization_barrier(jnp.mean(scaled, -1, keepdims=True))
    second = lax.optimization_barrier(jnp.mean(scaled * centred, -1, keepdims=True))
    return inverse * (scaled - first - centred * second)

def reference(acts, section_grads, gain, w_qkv, w_out, labels):
    section_total = acts.shape[0]
    level_count, row_count, col_count, width = acts.shape[1:]
    rolled_labels = jnp.roll(labels, (-SHIFT_LAT, -SHIFT_LON), (0, 1))
    label_field = jnp.broadcast_to(rolled_labels[None, :, :, None], (level_count, row_count, col_count, 1))
    label_win = to_windows(label_field)[..., 0]
    lat_windows = row_count // WIN_LAT
    lon_windows = col_count // WIN_LON
    token_count = level_count * WIN_LAT * WIN_LON
    outputs = []
    wo_blocks = []
    for section_index in range(section_total):
        upstream = section_grads[(section_index + 1) % section_total]
        rolled_input = jnp.roll(acts[section_index], (-SHIFT_LAT, -SHIFT_LON), (1, 2))
        rolled_grad = jnp.roll(upstream, (-SHIFT_LAT, -SHIFT_LON), (1, 2))
        normed, centred, inverse = normalize(rolled_input, gain[section_index])
        projected = jnp.dot(normed.reshape(-1, width), w_qkv[section_index], preferred_element_type=jnp.float32)
        projected = projected.astype(jnp.bfloat16).reshape(level_count, row_count, col_count, 3 * width)
        proj_groups = to_windows(projected).reshape(lat_windows, lon_windows, token_count, 3 * width)
        grad_groups = to_windows(rolled_grad).reshape(lat_windows, lon_windows, token_count, width)
        label_groups = label_win.reshape(lat_windows, lon_windows, token_count)
        weight_out = w_out[section_index]

        def one_row(items):
            return attend_backward(items[0], items[1], items[2], weight_out)
        grad_proj, attended = lax.map(one_row, (proj_groups, grad_groups, label_groups))
        grad_proj = from_windows(grad_proj.reshape(-1, token_count, 3 * width), level_count, row_count, col_count)
        attended = from_windows(attended.reshape(-1, token_count, width), level_count, row_count, col_count)
        wo_blocks.append(jnp.dot(attended.reshape(-1, width).T, rolled_grad.reshape(-1, width), preferred_element_type=jnp.float32))
        branch = norm_backward(grad_proj, w_qkv[section_index], gain[section_index], centred, inverse)
        summed = (rolled_grad.astype(jnp.float32) + branch).astype(jnp.bfloat16)
        outputs.append(jnp.roll(summed, (SHIFT_LAT, SHIFT_LON), (1, 2)))
    return (jnp.stack(outputs, 0), jnp.concatenate(wo_blocks, 0))
```

```python
import functools

import jax
import jax.numpy as jnp
import numpy as np
from jax import lax
from jax.experimental import pallas as pl
from jax.experimental.pallas import tpu as pltpu
from jax.sharding import PartitionSpec as P

MESH = pl.DeviceIdType.MESH
LEV = 2
LAT_CELLS = 6
LON_CELLS = 24
TOKENS = 288
WIN = 144
D = 512
GROUP = 256
HEADS = 4
COLS = HEADS * WIN
SEND = 320
R00 = (0, 112)
R10 = (112, 112)
R01 = (224, 48)
R11 = (272, 48)
epsilon = 1e-05
masked_score = -1e30
open_score = 3e38


def natural(lev, row, col):
    return (lev * LAT_CELLS + row) * LON_CELLS + col


def group_cells(upper, left, part):
    rows = range(0, 3) if upper else range(3, 6)
    if left:
        cols = range(0, 6)
    else:
        cols = range(6, 18) if part == 0 else range(18, 24)
    return [(l, r, c) for l in range(LEV) for r in rows for c in cols]


def layouts():
    sent = {}
    for name, upper, left, start in (("00", 0, 0, 0), ("10", 1, 0, 112), ("01", 0, 1, 224), ("11", 1, 1, 272)):
        at = start
        for part in range(1 if left else 2):
            for cell in group_cells(upper, left, part):
                sent[(name, part if not left else 1, cell)] = at
                at += 1
    p_send = np.zeros((SEND, TOKENS), np.float32)
    for (name, part, cell), at in sent.items():
        p_send[at, natural(*cell)] = 1
    order = []
    for name, upper, left, part in (
        ("00", 0, 0, 0),
        ("10", 1, 0, 0),
        ("00", 0, 0, 1),
        ("10", 1, 0, 1),
        ("01", 0, 1, 1),
        ("11", 1, 1, 1),
    ):
        for cell in group_cells(upper, left, part):
            order.append((name, part, cell))
    p_win = np.zeros((TOKENS, SEND), np.float32)
    rows = np.zeros((TOKENS, 24), np.float32)
    cols = np.zeros((TOKENS, 128), np.float32)
    for t, (name, part, cell) in enumerate(order):
        p_win[t, sent[(name, part, cell)]] = 1
        rows[t, cell[1] + (6 if name[0] == "1" else 0)] = 1
        cols[t, cell[2] + (24 if name[1] == "1" else 0)] = 1
    return p_send, p_win, rows, cols


def dot(left, right, dims=((1,), (0,))):
    return lax.dot_general(left, right, (dims, ((), ())), preferred_element_type=jnp.float32)


NT = ((1,), (1,))
TN = ((0,), (0,))


def kernel(
    sizes,
    acts_hbm, grads_hbm, gain_hbm, wqkv_hbm, wout_hbm, labels_hbm,
    psend_hbm, pwin_hbm, pret_hbm, pout_hbm, rows_hbm, cols_hbm,
    out_ref, wo_ref,
    acts_v, grads_v, gain_v, wqkv_v, wout_v, labels_v,
    psend_v, pwin_v, pret_v, pout_v, rows_v, cols_v,
    acts_send, acts_recv, grads_send, grads_recv, ret_send, ret_recv,
    mask_v, perm_v, qkv_v, qb_v, w_v, wl_v, att_v, up_v, ga_v, gb_v, gp_v, cen_v, inv_v,
    own_v, a_send, a_recv, b_send, b_recv, c_send, c_recv, d_send, d_recv,
    in_sem, send_sem, recv_sem,
):
    pipe_n, nx, ny, nz = sizes
    lon_n, lat_n = nx * ny, nz * 2
    s = lax.axis_index("pipe")
    j = lax.axis_index("lon")
    i = lax.axis_index("lat")
    x, y = j // ny, j % ny
    z, core = i // 2, i % 2

    def near(ds, dj, di):
        return (
            (s + ds + pipe_n) % pipe_n if ds else s,
            (j + dj + lon_n) % lon_n if dj else j,
            (i + di + lat_n) % lat_n if di else i,
        )

    def on_x(k):
        return (s, ((x + k) % nx) * ny + y, i)

    def on_y(k):
        return (s, x * ny + (y + k) % ny, i)

    twin = (s, j, z * 2 + (1 - core))
    far = (s, j, ((z + 1) % nz) * 2 + core)

    barrier = pltpu.get_barrier_semaphore()
    senders = [near(0, 0, 1), near(0, 1, 0), near(0, 1, 1), near(0, 0, -1), near(0, -1, 0), near(0, -1, -1)]
    senders += [near(1, 0, 0), near(1, 0, 1), near(1, 1, 0), near(1, 1, 1)]
    senders += [twin, far]
    senders += [on_x(k) for k in range(1, nx)] + [on_y(k) for k in range(1, ny)]
    for device in senders:
        pl.semaphore_signal(barrier, inc=1, device_id=device, device_id_type=MESH)

    loads = []
    for n, (src, dst) in enumerate((
        (acts_hbm, acts_v), (psend_hbm, psend_v), (grads_hbm, grads_v), (labels_hbm, labels_v),
        (rows_hbm, rows_v), (cols_hbm, cols_v), (pwin_hbm, pwin_v), (gain_hbm, gain_v),
        (wqkv_hbm, wqkv_v), (wout_hbm, wout_v), (pret_hbm, pret_v), (pout_hbm, pout_v),
    )):
        load = pltpu.make_async_copy(src, dst, in_sem.at[n])
        load.start()
        loads.append(load)
    (l_acts, l_psend, l_grads, l_labels, l_rows, l_cols, l_pwin, l_gain, l_wqkv, l_wout, l_pret, l_pout) = loads

    started = []

    def send(src, dst, device):
        n = len(started)
        copy = pltpu.make_async_remote_copy(
            src_ref=src, dst_ref=dst, send_sem=send_sem.at[n], recv_sem=recv_sem.at[n],
            device_id=device, device_id_type=MESH,
        )
        copy.start()
        started.append(copy)
        return copy

    def rows_of(ref, part):
        return ref.at[pl.ds(part[0], part[1])]

    l_acts.wait()
    l_psend.wait()
    ordered = dot(psend_v[...], acts_v[...]).astype(jnp.bfloat16)
    acts_send[...] = ordered
    acts_recv[0:112, :] = ordered[0:112]
    l_grads.wait()
    grads_send[...] = dot(psend_v[...], grads_v[...]).astype(jnp.bfloat16)

    pl.semaphore_wait(barrier, len(senders))
    acts_in = [
        send(rows_of(acts_send, R10), rows_of(acts_recv, R10), near(0, 0, -1)),
        send(rows_of(acts_send, R11), rows_of(acts_recv, R11), near(0, -1, -1)),
        send(rows_of(acts_send, R01), rows_of(acts_recv, R01), near(0, -1, 0)),
    ]
    grads_in = [
        send(rows_of(grads_send, R10), rows_of(grads_recv, R10), near(-1, 0, -1)),
        send(rows_of(grads_send, R11), rows_of(grads_recv, R11), near(-1, -1, -1)),
        send(rows_of(grads_send, R00), rows_of(grads_recv, R00), near(-1, 0, 0)),
        send(rows_of(grads_send, R01), rows_of(grads_recv, R01), near(-1, -1, 0)),
    ]

    l_labels.wait()
    l_rows.wait()
    l_cols.wait()
    row_n, col_n = labels_v.shape
    cell = lax.broadcasted_iota(jnp.int32, (col_n, 128), 0) - j * LON_CELLS
    cell = jnp.where(cell < 0, cell + col_n, cell)
    pick_col = (cell == lax.broadcasted_iota(jnp.int32, (col_n, 128), 1)).astype(jnp.float32)
    row = lax.broadcasted_iota(jnp.int32, (row_n, row_n), 1) - i * LAT_CELLS
    row = jnp.where(row < 0, row + row_n, row)
    pick_row = (row == lax.broadcasted_iota(jnp.int32, (row_n, row_n), 0)).astype(jnp.float32)
    near_labels = dot(pick_row, dot(labels_v[...].astype(jnp.float32), pick_col))
    token_label = jnp.sum(dot(rows_v[...], near_labels) * cols_v[...], -1, keepdims=True)
    lane = lax.broadcasted_iota(jnp.int32, (TOKENS, 128), 1).astype(jnp.float32)
    one_hot = (token_label == lane).astype(jnp.float32).astype(jnp.bfloat16)
    for w in range(2):
        here = one_hot[w * WIN:(w + 1) * WIN]
        alike = dot(here, jnp.concatenate([here] * HEADS, 0), NT)
        mask_v[w] = jnp.where(alike > 0.5, open_score, masked_score)

    per = D // (2 * nx * ny * nz)
    m = lax.broadcasted_iota(jnp.int32, (D, D), 0)
    r_at = m % per
    z_at = (m // per) % nz
    y_at = (m // (per * nz)) % ny
    x_at = (m // (per * nz * ny)) % nx
    c_at = m // (per * nz * ny * nx)
    feature = (
        (((x_at + x) % nx * ny + (y_at + y) % ny) * nz + (z_at + z) % nz) * 2 + (c_at + core) % 2
    ) * per + r_at
    perm_v[...] = (feature == lax.broadcasted_iota(jnp.int32, (D, D), 1)).astype(jnp.float32).astype(jnp.bfloat16)

    l_pwin.wait()
    l_gain.wait()
    l_wqkv.wait()
    for copy in acts_in:
        copy.wait_recv()
    gain = gain_v[...]
    inputs = dot(pwin_v[...], acts_recv[...])
    mean = jnp.mean(inputs, -1, keepdims=True)
    centred = inputs - mean
    inverse = 1.0 / jnp.sqrt(jnp.mean(centred * centred, -1, keepdims=True) + epsilon)
    centred = centred * inverse
    cen_v[...] = centred
    inv_v[...] = jnp.broadcast_to(inverse, inv_v.shape)
    projected = dot((centred * gain).astype(jnp.bfloat16), wqkv_v[...])
    for part in range(3):
        for w in range(2):
            for g in range(2):
                at = part * D + g * GROUP
                qkv_v[part, w * 2 + g] = projected[w * WIN:(w + 1) * WIN, at:at + GROUP].astype(jnp.bfloat16)

    head_lane = lax.broadcasted_iota(jnp.int32, (1, GROUP), 1) // 64
    head_mask = [(head_lane == h).astype(jnp.float32) for h in range(HEADS)]

    def spread(block, dst, n, scale):
        for h in range(HEADS):
            dst[n, h * WIN:(h + 1) * WIN, :] = (block * (head_mask[h] * scale)).astype(jnp.bfloat16)

    def gather(product):
        total = product[0:WIN] * head_mask[0]
        for h in range(1, HEADS):
            total = total + product[h * WIN:(h + 1) * WIN] * head_mask[h]
        return total

    def forward(n, carry):
        spread(qkv_v[0, n].astype(jnp.float32), qb_v, n, 0.125)
        scores = jnp.minimum(dot(qkv_v[1, n], qb_v[n], NT), mask_v[n // 2])
        exps = jnp.exp(scores - jnp.max(scores, 0, keepdims=True))
        weights = exps * (1.0 / jnp.sum(exps, 0, keepdims=True))
        w_v[n] = weights
        low = weights.astype(jnp.bfloat16)
        wl_v[n] = low
        att_v[n] = gather(dot(low, qkv_v[2, n], TN)).astype(jnp.bfloat16)
        return carry

    lax.fori_loop(0, 4, forward, 0)

    l_wout.wait()
    for copy in grads_in:
        copy.wait_recv()
    upstream = dot(pwin_v[...], grads_recv[...]).astype(jnp.bfloat16)
    up_v[...] = upstream
    attended = jnp.concatenate(
        [jnp.concatenate([att_v[2 * w], att_v[2 * w + 1]], 1) for w in range(2)], 0
    )
    turned = dot(perm_v[...], attended, NT).astype(jnp.bfloat16)
    half = D // 2
    a_send[...] = dot(turned[half:], upstream).astype(jnp.bfloat16)
    step_a = send(a_send, a_recv, twin)
    own_v[...] = dot(turned[:half], upstream)

    grad_att = dot(upstream, wout_v[...], NT)
    for w in range(2):
        for g in range(2):
            ga_v[w * 2 + g] = grad_att[w * WIN:(w + 1) * WIN, g * GROUP:(g + 1) * GROUP].astype(jnp.bfloat16)

    def backward(n, carry):
        spread(ga_v[n].astype(jnp.float32), gb_v, n, 1.0)
        grad_w = dot(qkv_v[2, n], gb_v[n], NT)
        weights = w_v[n]
        inner = jnp.sum(grad_w * weights, 0, keepdims=True)
        grad_s = (weights * (grad_w - inner)).astype(jnp.bfloat16)
        gp_v[0, n] = (gather(dot(grad_s, qkv_v[1, n], TN)) * 0.125).astype(jnp.bfloat16)
        gp_v[1, n] = dot(grad_s, qb_v[n]).astype(jnp.bfloat16)
        gp_v[2, n] = dot(wl_v[n], gb_v[n]).astype(jnp.bfloat16)
        return carry

    lax.fori_loop(0, 2, backward, 0)

    step_a.wait_recv()
    chunk = half // nx
    summed = own_v[...] + a_recv[...].astype(jnp.float32)
    own_v[...] = summed
    b_send[...] = summed.astype(jnp.bfloat16)
    step_b = [
        send(b_send.at[pl.ds(k * chunk, chunk)], b_recv.at[pl.ds((k - 1) * chunk, chunk)], on_x(k))
        for k in range(1, nx)
    ]

    lax.fori_loop(2, 4, backward, 0)

    for copy in step_b:
        copy.wait_recv()
    total = own_v[0:chunk, :]
    for k in range(1, nx):
        total = total + b_recv[(k - 1) * chunk:k * chunk, :].astype(jnp.float32)
    own_v[0:chunk, :] = total
    piece = chunk // ny
    for k in range(1, ny):
        part = total[k * piece:(k + 1) * piece]
        c_send[k] = jnp.concatenate([part[:, :half], part[:, half:]], 0).astype(jnp.bfloat16)
    step_c = [send(c_send.at[k], c_recv.at[k], on_y(k)) for k in range(1, ny)]

    grad_proj = jnp.concatenate(
        [
            jnp.concatenate([gp_v[part, 2 * w + g] for part in range(3) for g in range(2)], 1)
            for w in range(2)
        ],
        0,
    )
    scaled = dot(grad_proj, wqkv_v[...], NT) * gain
    centred = cen_v[...]
    first = jnp.mean(scaled, -1, keepdims=True)
    second = jnp.mean(scaled * centred, -1, keepdims=True)
    branch = inv_v[:, 0:1] * (scaled - first - centred * second)
    result = (up_v[...].astype(jnp.float32) + branch).astype(jnp.bfloat16)
    l_pret.wait()
    back = dot(pret_v[...], result).astype(jnp.bfloat16)
    ret_send[...] = back
    ret_recv[0:112, :] = back[0:112]
    ret_in = [
        send(rows_of(ret_send, R10), rows_of(ret_recv, R10), near(0, 0, 1)),
        send(rows_of(ret_send, R11), rows_of(ret_recv, R11), near(0, 1, 1)),
        send(rows_of(ret_send, R01), rows_of(ret_recv, R01), near(0, 1, 0)),
    ]

    for copy in step_c:
        copy.wait_recv()
    total = own_v[0:piece, :]
    for k in range(1, ny):
        got = c_recv[k].astype(jnp.float32)
        total = total + jnp.concatenate([got[:piece], got[piece:]], 1)
    d_send[...] = total[per:]
    step_d = send(d_send, d_recv, far)

    l_pout.wait()
    for copy in ret_in:
        copy.wait_recv()
    out_ref[...] = dot(pout_v[...], ret_recv[...]).astype(jnp.bfloat16)
    step_d.wait_recv()
    wo_ref[...] = total[:per] + d_recv[...]
    for copy in started:
        copy.wait_send()


def on_device(sizes, acts, section_grads, gain, w_qkv, w_out, labels):
    pipe_n, nx, ny, nz = sizes
    p_send, p_win, rows, cols = layouts()
    low = lambda m: jnp.asarray(m, jnp.bfloat16)
    per = D // (2 * nx * ny * nz)
    half = D // 2
    chunk = half // nx
    piece = chunk // ny
    sends = 3 + 4 + 3 + 1 + (nx - 1) + (ny - 1) + 1
    bf, f32 = jnp.bfloat16, jnp.float32
    vm = pltpu.VMEM
    scratch = [
        vm((TOKENS, D), bf), vm((TOKENS, D), bf), vm((1, D), f32), vm((D, 3 * D), bf), vm((D, D), bf),
        vm(labels.shape, jnp.int32),
        vm((SEND, TOKENS), bf), vm((TOKENS, SEND), bf), vm((SEND, TOKENS), bf), vm((TOKENS, SEND), bf),
        vm((TOKENS, 24), f32), vm((TOKENS, 128), f32),
    ]
    scratch += [vm((SEND, D), bf)] * 6
    scratch += [
        vm((2, WIN, COLS), f32), vm((D, D), bf), vm((3, 4, WIN, GROUP), bf), vm((4, COLS, GROUP), bf),
        vm((4, WIN, COLS), f32), vm((4, WIN, COLS), bf), vm((4, WIN, GROUP), bf), vm((TOKENS, D), bf),
        vm((4, WIN, GROUP), bf), vm((4, COLS, GROUP), bf), vm((3, 4, WIN, GROUP), bf),
        vm((TOKENS, D), f32), vm((TOKENS, 128), f32),
    ]
    scratch += [
        vm((half, D), f32), vm((half, D), bf), vm((half, D), bf), vm((half, D), bf),
        vm(((nx - 1) * chunk, D), bf), vm((ny, 2 * piece, half), bf), vm((ny, 2 * piece, half), bf),
        vm((per, D), f32), vm((per, D), f32),
        pltpu.SemaphoreType.DMA((12,)), pltpu.SemaphoreType.DMA((sends,)), pltpu.SemaphoreType.DMA((sends,)),
    ]
    anywhere = pl.BlockSpec(memory_space=pl.ANY)
    out, wo = pl.pallas_call(
        functools.partial(kernel, sizes),
        out_shape=(jax.ShapeDtypeStruct((TOKENS, D), bf), jax.ShapeDtypeStruct((per, D), f32)),
        in_specs=[anywhere] * 12,
        out_specs=(pl.BlockSpec(memory_space=pltpu.VMEM), pl.BlockSpec(memory_space=pltpu.VMEM)),
        scratch_shapes=scratch,
        compiler_params=pltpu.CompilerParams(
            collective_id=0, has_side_effects=True, vmem_limit_bytes=48 * 1024 * 1024
        ),
        name="sublayer",
    )(
        acts.reshape(TOKENS, D), section_grads.reshape(TOKENS, D), gain, w_qkv[0], w_out[0], labels,
        low(p_send), low(p_win), low(p_win.T), low(p_send.T), jnp.asarray(rows), jnp.asarray(cols),
    )
    return out.reshape(acts.shape), wo


def solution(mesh):
    pipe_n, lon_n, lat_n = (mesh.shape[axis] for axis in ("pipe", "lon", "lat"))
    ny = 8 if lon_n == 32 else min(lon_n, 2)
    sizes = (pipe_n, lon_n // ny, ny, lat_n // 2)
    in_specs = (
        P("pipe", None, "lat", "lon", None),
        P("pipe", None, "lat", "lon", None),
        P("pipe", None),
        P("pipe", None, None),
        P("pipe", None, None),
        P(),
    )
    out_specs = (P("pipe", None, "lat", "lon", None), P(("pipe", "lon", "lat"), None))
    return jax.shard_map(
        functools.partial(on_device, sizes), mesh=mesh, in_specs=in_specs, out_specs=out_specs, check_vma=False
    )
```

```python
import functools

import jax
import jax.numpy as jnp
import numpy as np
from jax import lax
from jax.experimental import pallas as pl
from jax.experimental.pallas import tpu as pltpu
from jax.sharding import PartitionSpec as P

MESH = pl.DeviceIdType.MESH
LEV = 2
LAT_CELLS = 6
LON_CELLS = 24
TOKENS = 288
WIN = 144
D = 512
GROUP = 256
HEADS = 4
COLS = HEADS * WIN
PART_AT = {"00": 0, "10": 112, "01": 224, "11": 272}
PART_ROWS = 320
ACTS_AT = {"own": 0, "10": 288, "01": 400, "11": 448}
ACTS_ROWS = 496
SIZE = {"00": 112, "10": 112, "01": 48, "11": 48}
epsilon = 1e-05
masked_score = -1e30
open_score = 3e38


def natural(lev, row, col):
    return (lev * LAT_CELLS + row) * LON_CELLS + col


def cells(group, part):
    rows = range(0, 3) if group[0] == "1" else range(3, 6)
    if group[1] == "1":
        cols = range(0, 6) if part == 1 else ()
    else:
        cols = range(6, 18) if part == 0 else range(18, 24)
    return [(l, r, c) for l in range(LEV) for r in rows for c in cols]


def layouts():
    groups = ("00", "10", "01", "11")
    place = {g: {cell: n for n, cell in enumerate(cells(g, 0) + cells(g, 1))} for g in groups}

    part = np.zeros((PART_ROWS, TOKENS), np.float32)
    acts_win = np.zeros((TOKENS, ACTS_ROWS), np.float32)
    part_win = np.zeros((TOKENS, PART_ROWS), np.float32)
    rows = np.zeros((TOKENS, 24), np.float32)
    cols = np.zeros((TOKENS, 128), np.float32)
    order = [(g, cell) for w in range(2) for g in groups for cell in cells(g, w)]
    for t, (g, cell) in enumerate(order):
        n = place[g][cell]
        part[PART_AT[g] + n, natural(*cell)] = 1
        part_win[t, PART_AT[g] + n] = 1
        acts_win[t, natural(*cell) if g == "00" else ACTS_AT[g] + n] = 1
        rows[t, cell[1] + (6 if g[0] == "1" else 0)] = 1
        cols[t, cell[2] + (24 if g[1] == "1" else 0)] = 1
    return part, acts_win, part_win, part_win.T, part.T, rows, cols


def regroup(pieces, per):
    old = np.arange(4 * pieces * per).reshape(4, pieces, per).transpose(1, 0, 2).reshape(-1)
    matrix = np.zeros((old.size, old.size), np.float32)
    matrix[np.arange(old.size), old] = 1
    return matrix


def dot(left, right, dims=((1,), (0,))):
    return lax.dot_general(left, right, (dims, ((), ())), preferred_element_type=jnp.float32)


NT = ((1,), (1,))
TN = ((0,), (0,))


def kernel(
    sizes,
    acts_hbm, grads_hbm, gain_hbm, wqkv_hbm, wout_hbm, labels_hbm,
    part_hbm, awin_hbm, gwin_hbm, back_hbm, home_hbm, rows_hbm, cols_hbm, regroup_hbm,
    out_ref, wo_ref,
    acts_buf, grads_v, gain_v, wqkv_v, wout_v, labels_v,
    part_v, awin_v, gwin_v, back_v, home_v, rows_v, cols_v, regroup_v,
    acts_part, grads_part, grads_buf, ret_send, ret_recv,
    mask_v, perm_v, qkv_v, qb_v, w_v, wl_v, att_v, up_v, ga_v, gb_v, gp_v, cen_v, inv_v,
    own_v, a_send, a_recv, b_send, b_recv, c_send, c_recv,
    in_sem, send_sem, recv_sem, ready_sem,
):
    pipe_n, nx, ny, nz = sizes
    lon_n, lat_n = nx * ny, nz * 2
    s = lax.axis_index("pipe")
    j = lax.axis_index("lon")
    i = lax.axis_index("lat")
    x, y = j // ny, j % ny
    z, core = i // 2, i % 2

    def near(ds, dj, di):
        return (
            (s + ds + pipe_n) % pipe_n if ds else s,
            (j + dj + lon_n) % lon_n if dj else j,
            (i + di + lat_n) % lat_n if di else i,
        )

    def on_x(k):
        return (s, ((x + k) % nx) * ny + y, i)

    def on_yz(k):
        return (s, x * ny + (y + k // nz) % ny, (z + k % nz) % nz * 2 + core)

    twin = (s, j, z * 2 + (1 - core))

    barrier = pltpu.get_barrier_semaphore()
    greeted = [near(0, 0, 1), near(0, 1, 0), near(0, 1, 1), near(0, 0, -1), near(0, -1, 0), near(0, -1, -1), twin]
    greeted += [on_x(k) for k in range(1, nx)] + [on_yz(k) for k in range(1, ny * nz)]
    before = [near(-1, 0, 0), near(-1, 0, -1), near(-1, -1, 0), near(-1, -1, -1)]
    after = [near(1, 0, 0), near(1, 0, 1), near(1, 1, 0), near(1, 1, 1)]
    last = pipe_n - 1

    def greet(devices):
        for device in devices:
            pl.semaphore_signal(barrier, inc=1, device_id=device, device_id_type=MESH)

    @pl.when(s != last)
    def _():
        greet(after)

    @pl.when(s == 0)
    def _():
        greet(before)

    greet(greeted)

    loads = []
    for n, (src, dst) in enumerate((
        (acts_hbm, acts_buf.at[pl.ds(0, TOKENS)]), (part_hbm, part_v), (grads_hbm, grads_v), (labels_hbm, labels_v),
        (rows_hbm, rows_v), (cols_hbm, cols_v), (awin_hbm, awin_v), (gain_hbm, gain_v),
        (wqkv_hbm, wqkv_v), (gwin_hbm, gwin_v), (wout_hbm, wout_v), (regroup_hbm, regroup_v),
        (back_hbm, back_v), (home_hbm, home_v),
    )):
        load = pltpu.make_async_copy(src, dst, in_sem.at[n])
        load.start()
        loads.append(load)
    (
        l_acts, l_part, l_grads, l_labels, l_rows, l_cols, l_awin, l_gain,
        l_wqkv, l_gwin, l_wout, l_regroup, l_back, l_home,
    ) = loads

    planned = []

    def plan(src, dst, device):
        n = len(planned)
        copy = pltpu.make_async_remote_copy(
            src_ref=src, dst_ref=dst, send_sem=send_sem.at[n], recv_sem=recv_sem.at[n],
            device_id=device, device_id_type=MESH,
        )
        planned.append(copy)
        return copy

    def send(src, dst, device):
        copy = plan(src, dst, device)
        copy.start()
        return copy

    def block(ref, at, size):
        return ref.at[pl.ds(at, size)]

    here = {"10": (0, -1), "11": (-1, -1), "00": (0, 0), "01": (-1, 0)}
    acts_in = [
        plan(block(acts_part, PART_AT[g] - 112, SIZE[g]), block(acts_buf, ACTS_AT[g], SIZE[g]), near(0, *here[g]))
        for g in ("10", "11", "01")
    ]
    grads_in = [
        plan(block(grads_part, PART_AT[g], SIZE[g]), block(grads_buf, PART_AT[g], SIZE[g]), near(-1, *here[g]))
        for g in ("10", "11", "00", "01")
    ]

    l_acts.wait()
    l_part.wait()
    acts_part[...] = dot(part_v[112:], acts_buf[0:TOKENS]).astype(jnp.bfloat16)
    pl.semaphore_wait(barrier, len(greeted) + jnp.where(s > 0, 4, 0) + jnp.where(s == last, 4, 0))

    @pl.when(s == last)
    def _():
        for device in after:
            pl.semaphore_signal(ready_sem, inc=1, device_id=device, device_id_type=MESH)

    for copy in acts_in:
        copy.start()
    l_grads.wait()
    grads_part[...] = dot(part_v[...], grads_v[...]).astype(jnp.bfloat16)

    @pl.when(s != 0)
    def _():
        for copy in grads_in:
            copy.start()

    l_labels.wait()
    l_rows.wait()
    l_cols.wait()
    row_n, col_n = labels_v.shape
    cell = lax.broadcasted_iota(jnp.int32, (col_n, 128), 0) - j * LON_CELLS
    cell = jnp.where(cell < 0, cell + col_n, cell)
    pick_col = (cell == lax.broadcasted_iota(jnp.int32, (col_n, 128), 1)).astype(jnp.float32)
    row = lax.broadcasted_iota(jnp.int32, (row_n, row_n), 1) - i * LAT_CELLS
    row = jnp.where(row < 0, row + row_n, row)
    pick_row = (row == lax.broadcasted_iota(jnp.int32, (row_n, row_n), 0)).astype(jnp.float32)
    near_labels = dot(pick_row, dot(labels_v[...].astype(jnp.float32), pick_col))
    token_label = jnp.sum(dot(rows_v[...], near_labels) * cols_v[...], -1, keepdims=True)
    lane = lax.broadcasted_iota(jnp.int32, (TOKENS, 128), 1).astype(jnp.float32)
    one_hot = (token_label == lane).astype(jnp.float32).astype(jnp.bfloat16)
    for w in range(2):
        here = one_hot[w * WIN:(w + 1) * WIN]
        alike = dot(here, jnp.concatenate([here] * HEADS, 0), NT)
        mask_v[w] = jnp.where(alike > 0.5, open_score, masked_score)

    per = D // (2 * nx * ny * nz)
    m = lax.broadcasted_iota(jnp.int32, (D, D), 0)
    r_at = m % per
    z_at = (m // per) % nz
    y_at = (m // (per * nz)) % ny
    x_at = (m // (per * nz * ny)) % nx
    c_at = m // (per * nz * ny * nx)
    feature = (
        (((x_at + x) % nx * ny + (y_at + y) % ny) * nz + (z_at + z) % nz) * 2 + (c_at + core) % 2
    ) * per + r_at
    perm_v[...] = (feature == lax.broadcasted_iota(jnp.int32, (D, D), 1)).astype(jnp.float32).astype(jnp.bfloat16)

    l_awin.wait()
    l_gain.wait()
    l_wqkv.wait()
    for copy in acts_in:
        copy.wait_recv()
    gain = gain_v[...]
    inputs = dot(awin_v[...], acts_buf[...])
    mean = jnp.mean(inputs, -1, keepdims=True)
    centred = inputs - mean
    inverse = 1.0 / jnp.sqrt(jnp.mean(centred * centred, -1, keepdims=True) + epsilon)
    centred = centred * inverse
    cen_v[...] = centred
    inv_v[...] = jnp.broadcast_to(inverse, inv_v.shape)
    projected = dot((centred * gain).astype(jnp.bfloat16), wqkv_v[...])
    for part in range(3):
        for w in range(2):
            for g in range(2):
                at = part * D + g * GROUP
                qkv_v[part, w * 2 + g] = projected[w * WIN:(w + 1) * WIN, at:at + GROUP].astype(jnp.bfloat16)

    head_lane = lax.broadcasted_iota(jnp.int32, (1, GROUP), 1) // 64
    head_mask = [(head_lane == h).astype(jnp.float32) for h in range(HEADS)]

    def spread(block, dst, n, scale):
        for h in range(HEADS):
            dst[n, h * WIN:(h + 1) * WIN, :] = (block * (head_mask[h] * scale)).astype(jnp.bfloat16)

    def gather(product):
        total = product[0:WIN] * head_mask[0]
        for h in range(1, HEADS):
            total = total + product[h * WIN:(h + 1) * WIN] * head_mask[h]
        return total

    def forward(n, carry):
        spread(qkv_v[0, n].astype(jnp.float32), qb_v, n, 0.125)
        scores = jnp.minimum(dot(qkv_v[1, n], qb_v[n], NT), mask_v[n // 2])
        exps = jnp.exp(scores - jnp.max(scores, 0, keepdims=True))
        weights = exps * (1.0 / jnp.sum(exps, 0, keepdims=True))
        w_v[n] = weights
        low = weights.astype(jnp.bfloat16)
        wl_v[n] = low
        att_v[n] = gather(dot(low, qkv_v[2, n], TN)).astype(jnp.bfloat16)
        return carry

    @pl.when(s == 0)
    def _():
        pl.semaphore_wait(ready_sem, 4)
        for copy in grads_in:
            copy.start()

    lax.fori_loop(0, 4, forward, 0)

    l_wout.wait()
    l_gwin.wait()
    for copy in grads_in:
        copy.wait_recv()
    upstream = dot(gwin_v[...], grads_buf[...]).astype(jnp.bfloat16)
    up_v[...] = upstream
    attended = jnp.concatenate(
        [jnp.concatenate([att_v[2 * w], att_v[2 * w + 1]], 1) for w in range(2)], 0
    )
    turned = dot(perm_v[...], attended, NT).astype(jnp.bfloat16)
    half = D // 2
    a_send[...] = dot(turned[half:], upstream).astype(jnp.bfloat16)
    step_a = send(a_send, a_recv, twin)
    own_v[...] = dot(turned[:half], upstream)

    grad_att = dot(upstream, wout_v[...], NT)
    for w in range(2):
        for g in range(2):
            ga_v[w * 2 + g] = grad_att[w * WIN:(w + 1) * WIN, g * GROUP:(g + 1) * GROUP].astype(jnp.bfloat16)

    def backward(n, carry):
        spread(ga_v[n].astype(jnp.float32), gb_v, n, 1.0)
        grad_w = dot(qkv_v[2, n], gb_v[n], NT)
        weights = w_v[n]
        inner = jnp.sum(grad_w * weights, 0, keepdims=True)
        grad_s = (weights * (grad_w - inner)).astype(jnp.bfloat16)
        gp_v[0, n] = (gather(dot(grad_s, qkv_v[1, n], TN)) * 0.125).astype(jnp.bfloat16)
        gp_v[1, n] = dot(grad_s, qb_v[n]).astype(jnp.bfloat16)
        gp_v[2, n] = dot(wl_v[n], gb_v[n]).astype(jnp.bfloat16)
        return carry

    lax.fori_loop(0, 2, backward, 0)

    step_a.wait_recv()
    chunk = half // nx
    summed = own_v[...] + a_recv[...].astype(jnp.float32)
    own_v[...] = summed
    b_send[...] = summed.astype(jnp.bfloat16)
    step_b = [
        send(b_send.at[pl.ds(k * chunk, chunk)], b_recv.at[pl.ds((k - 1) * chunk, chunk)], on_x(k))
        for k in range(1, nx)
    ]

    lax.fori_loop(2, 4, backward, 0)

    grad_proj = jnp.concatenate(
        [
            jnp.concatenate([gp_v[part, 2 * w + g] for part in range(3) for g in range(2)], 1)
            for w in range(2)
        ],
        0,
    )
    scaled = dot(grad_proj, wqkv_v[...], NT) * gain
    centred = cen_v[...]
    first = jnp.mean(scaled, -1, keepdims=True)
    second = jnp.mean(scaled * centred, -1, keepdims=True)
    branch = inv_v[:, 0:1] * (scaled - first - centred * second)
    result = (up_v[...].astype(jnp.float32) + branch).astype(jnp.bfloat16)
    for copy in step_b:
        copy.wait_recv()
    total = own_v[0:chunk, :]
    for k in range(1, nx):
        total = total + b_recv[(k - 1) * chunk:k * chunk, :].astype(jnp.float32)
    own_v[0:chunk, :] = total
    l_regroup.wait()
    low = total.astype(jnp.bfloat16)
    stacked = jnp.concatenate([low[:, q * 128:(q + 1) * 128] for q in range(4)], 0)
    c_send[...] = dot(regroup_v[...], stacked).astype(jnp.bfloat16)
    size = 4 * per
    step_c = [
        send(block(c_send, k * size, size), block(c_recv, k * size, size), on_yz(k)) for k in range(1, ny * nz)
    ]

    l_back.wait()
    back = dot(back_v[...], result).astype(jnp.bfloat16)
    ret_send[...] = back
    ret_recv[0:112, :] = back[0:112]
    ret_in = [
        send(block(ret_send, PART_AT[g], SIZE[g]), block(ret_recv, PART_AT[g], SIZE[g]), device)
        for g, device in (("10", near(0, 0, 1)), ("11", near(0, 1, 1)), ("01", near(0, 1, 0)))
    ]

    for copy in step_c:
        copy.wait_recv()
    got = c_recv[size:2 * size].astype(jnp.float32)
    for k in range(2, ny * nz):
        got = got + c_recv[k * size:(k + 1) * size].astype(jnp.float32)
    wo_ref[...] = own_v[0:per, :] + jnp.concatenate([got[q * per:(q + 1) * per] for q in range(4)], 1)

    l_home.wait()
    for copy in ret_in:
        copy.wait_recv()
    out_ref[...] = dot(home_v[...], ret_recv[...]).astype(jnp.bfloat16)
    for copy in planned:
        copy.wait_send()


def on_device(sizes, acts, section_grads, gain, w_qkv, w_out, labels):
    pipe_n, nx, ny, nz = sizes
    per = D // (2 * nx * ny * nz)
    half = D // 2
    chunk = half // nx
    bf, f32 = jnp.bfloat16, jnp.float32
    part, acts_win, part_win, back, home, rows, cols = layouts()
    tables = [jnp.asarray(m, bf) for m in (part, acts_win, part_win, back, home)]
    tables += [jnp.asarray(rows), jnp.asarray(cols), jnp.asarray(regroup(ny * nz, per), bf)]
    sends = 3 + 4 + 3 + 1 + (nx - 1) + (ny * nz - 1)
    vm = pltpu.VMEM
    scratch = [
        vm((ACTS_ROWS, D), bf), vm((TOKENS, D), bf), vm((1, D), f32), vm((D, 3 * D), bf), vm((D, D), bf),
        vm(labels.shape, jnp.int32),
    ]
    scratch += [vm(m.shape, m.dtype) for m in tables]
    scratch += [
        vm((PART_ROWS - 112, D), bf), vm((PART_ROWS, D), bf), vm((PART_ROWS, D), bf), vm((PART_ROWS, D), bf), vm((PART_ROWS, D), bf),
    ]
    scratch += [
        vm((2, WIN, COLS), f32), vm((D, D), bf), vm((3, 4, WIN, GROUP), bf), vm((4, COLS, GROUP), bf),
        vm((4, WIN, COLS), f32), vm((4, WIN, COLS), bf), vm((4, WIN, GROUP), bf), vm((TOKENS, D), bf),
        vm((4, WIN, GROUP), bf), vm((4, COLS, GROUP), bf), vm((3, 4, WIN, GROUP), bf),
        vm((TOKENS, D), f32), vm((TOKENS, 128), f32),
    ]
    scratch += [
        vm((half, D), f32), vm((half, D), bf), vm((half, D), bf), vm((half, D), bf),
        vm((max(nx - 1, 1) * chunk, D), bf), vm((4 * chunk, 128), bf), vm((4 * chunk, 128), bf),
        pltpu.SemaphoreType.DMA((6 + len(tables),)),
        pltpu.SemaphoreType.DMA((sends,)), pltpu.SemaphoreType.DMA((sends,)), pltpu.SemaphoreType.REGULAR,
    ]
    anywhere = pl.BlockSpec(memory_space=pltpu.HBM)
    out, wo = pl.pallas_call(
        functools.partial(kernel, sizes),
        out_shape=(jax.ShapeDtypeStruct((TOKENS, D), bf), jax.ShapeDtypeStruct((per, D), f32)),
        in_specs=[anywhere] * (6 + len(tables)),
        out_specs=(pl.BlockSpec(memory_space=pltpu.VMEM), pl.BlockSpec(memory_space=pltpu.VMEM)),
        scratch_shapes=scratch,
        compiler_params=pltpu.CompilerParams(
            collective_id=0, has_side_effects=True, vmem_limit_bytes=60 * 1024 * 1024
        ),
        name="sublayer",
    )(
        acts.reshape(TOKENS, D), section_grads.reshape(TOKENS, D), gain, w_qkv[0], w_out[0], labels,
        *tables,
    )
    return out.reshape(acts.shape), wo


def solution(mesh):
    pipe_n, lon_n, lat_n = (mesh.shape[axis] for axis in ("pipe", "lon", "lat"))
    ny = 8 if lon_n == 32 else min(lon_n, 2)
    sizes = (pipe_n, lon_n // ny, ny, lat_n // 2)
    in_specs = (
        P("pipe", None, "lat", "lon", None),
        P("pipe", None, "lat", "lon", None),
        P("pipe", None),
        P("pipe", None, None),
        P("pipe", None, None),
        P(),
    )
    out_specs = (P("pipe", None, "lat", "lon", None), P(("pipe", "lon", "lat"), None))
    return jax.shard_map(
        functools.partial(on_device, sizes), mesh=mesh, in_specs=in_specs, out_specs=out_specs, check_vma=False
    )
```

```python
import functools

import jax
import jax.numpy as jnp
import numpy as np
from jax import lax
from jax.experimental import pallas as pl
from jax.experimental.pallas import tpu as pltpu
from jax.sharding import PartitionSpec as P

MESH = pl.DeviceIdType.MESH
LEV = 2
LAT_CELLS = 6
LON_CELLS = 24
TOKENS = 288
WIN = 144
D = 512
GROUP = 256
HEADS = 4
COLS = HEADS * WIN
PART_AT = {"00": 0, "10": 112, "01": 224, "11": 272}
PART_ROWS = 320
ACTS_AT = {"own": 0, "10": 288, "01": 400, "11": 448}
ACTS_ROWS = 496
SIZE = {"00": 112, "10": 112, "01": 48, "11": 48}
epsilon = 1e-05
masked_score = -1e30
open_score = 3e38


def natural(lev, row, col):
    return (lev * LAT_CELLS + row) * LON_CELLS + col


def cells(group, part):
    rows = range(0, 3) if group[0] == "1" else range(3, 6)
    if group[1] == "1":
        cols = range(0, 6) if part == 1 else ()
    else:
        cols = range(6, 18) if part == 0 else range(18, 24)
    return [(l, r, c) for l in range(LEV) for r in rows for c in cols]


def layouts():
    groups = ("00", "10", "01", "11")
    place = {g: {cell: n for n, cell in enumerate(cells(g, 0) + cells(g, 1))} for g in groups}

    table = np.full((PART_ROWS, 8), -1, np.int32)
    order = [(g, cell) for w in range(2) for g in groups for cell in cells(g, w)]
    for t, (g, cell) in enumerate(order):
        n = place[g][cell]
        table[PART_AT[g] + n, 0] = natural(*cell)
        table[PART_AT[g] + n, 1] = t
        table[t, 2] = natural(*cell) if g == "00" else ACTS_AT[g] + n
        table[t, 3] = PART_AT[g] + n
        table[natural(*cell), 4] = PART_AT[g] + n
        table[t, 5] = cell[1] + (6 if g[0] == "1" else 0)
        table[t, 6] = cell[2] + (24 if g[1] == "1" else 0)
    return table


def dot(left, right, dims=((1,), (0,))):
    return lax.dot_general(left, right, (dims, ((), ())), preferred_element_type=jnp.float32)


NT = ((1,), (1,))
TN = ((0,), (0,))


def kernel(
    sizes,
    acts_hbm, grads_hbm, gain_hbm, wqkv_hbm, wout_hbm, labels_hbm,
    table_hbm,
    out_ref, wo_ref,
    acts_buf, grads_v, gain_v, wqkv_v, wout_v, labels_v,
    table_v,
    part_v, awin_v, gwin_v, back_v, home_v, regroup_v,
    acts_part, grads_part, grads_buf, ret_send, ret_recv,
    mask_v, perm_v, qkv_v, qb_v, w_v, wl_v, att_v, up_v, ga_v, gb_v, gp_v, cen_v, inv_v,
    own_v, a_send, a_recv, b_send, b_recv, c_send, c_recv,
    in_sem, send_sem, recv_sem, ready_sem, across_sem,
):
    pipe_n, nx, ny, nz = sizes
    lon_n, lat_n = nx * ny, nz * 2
    s = lax.axis_index("pipe")
    j = lax.axis_index("lon")
    i = lax.axis_index("lat")
    x, y = j // ny, j % ny
    z, core = i // 2, i % 2

    def near(ds, dj, di):
        return (
            (s + ds + pipe_n) % pipe_n if ds else s,
            (j + dj + lon_n) % lon_n if dj else j,
            (i + di + lat_n) % lat_n if di else i,
        )

    def on_x(k):
        return (s, ((x + k) % nx) * ny + y, i)

    def on_yz(k):
        return (s, x * ny + (y + k // nz) % ny, (z + k % nz) % nz * 2 + core)

    twin = (s, j, z * 2 + (1 - core))

    barrier = pltpu.get_barrier_semaphore()
    greeted = [near(0, 0, 1), near(0, 1, 0), near(0, 1, 1), near(0, 0, -1), near(0, -1, 0), near(0, -1, -1), twin]
    greeted += [on_x(k) for k in range(1, nx)] + [on_yz(k * nz) for k in range(1, ny)]
    across = [on_yz(k * nz + 1) for k in range(ny)]
    before = [near(-1, 0, 0), near(-1, 0, -1), near(-1, -1, 0), near(-1, -1, -1)]
    after = [near(1, 0, 0), near(1, 0, 1), near(1, 1, 0), near(1, 1, 1)]
    last = pipe_n - 1

    def greet(devices):
        for device in devices:
            pl.semaphore_signal(barrier, inc=1, device_id=device, device_id_type=MESH)

    greet(greeted)

    @pl.when(s != last)
    def _():
        greet(after)

    @pl.when(s == 0)
    def _():
        greet(before)

    @pl.when(z == 0)
    def _():
        greet(across)


    loads = []
    for n, (src, dst) in enumerate((
        (table_hbm, table_v), (acts_hbm, acts_buf.at[pl.ds(0, TOKENS)]), (grads_hbm, grads_v), (labels_hbm, labels_v),
        (gain_hbm, gain_v), (wqkv_hbm, wqkv_v), (wout_hbm, wout_v),
    )):
        load = pltpu.make_async_copy(src, dst, in_sem.at[n])
        load.start()
        loads.append(load)
    l_table, l_acts, l_grads, l_labels, l_gain, l_wqkv, l_wout = loads

    def picks(column, rows, cols):
        found = table_v[0:rows, column:column + 1] == lax.broadcasted_iota(jnp.int32, (rows, cols), 1)
        return found.astype(jnp.float32)

    planned = []

    def plan(src, dst, device):
        n = len(planned)
        copy = pltpu.make_async_remote_copy(
            src_ref=src, dst_ref=dst, send_sem=send_sem.at[n], recv_sem=recv_sem.at[n],
            device_id=device, device_id_type=MESH,
        )
        planned.append(copy)
        return copy

    def send(src, dst, device):
        copy = plan(src, dst, device)
        copy.start()
        return copy

    def block(ref, at, size):
        return ref.at[pl.ds(at, size)]

    here = {"10": (0, -1), "11": (-1, -1), "00": (0, 0), "01": (-1, 0)}
    acts_in = [
        plan(block(acts_part, PART_AT[g] - 112, SIZE[g]), block(acts_buf, ACTS_AT[g], SIZE[g]), near(0, *here[g]))
        for g in ("10", "11", "01")
    ]
    grads_in = [
        plan(block(grads_part, PART_AT[g], SIZE[g]), block(grads_buf, PART_AT[g], SIZE[g]), near(-1, *here[g]))
        for g in ("10", "11", "00", "01")
    ]

    l_table.wait()
    part_v[...] = picks(0, PART_ROWS, TOKENS).astype(jnp.bfloat16)
    l_acts.wait()
    acts_part[...] = dot(part_v[112:], acts_buf[0:TOKENS]).astype(jnp.bfloat16)
    pl.semaphore_wait(barrier, len(greeted) + jnp.where(s > 0, 4, 0) + jnp.where(s == last, 4, 0) + jnp.where(z > 0, ny, 0))

    @pl.when(s == last)
    def _():
        for device in after:
            pl.semaphore_signal(ready_sem, inc=1, device_id=device, device_id_type=MESH)

    @pl.when(z > 0)
    def _():
        for device in across:
            pl.semaphore_signal(across_sem, inc=1, device_id=device, device_id_type=MESH)

    for copy in acts_in:
        copy.start()
    l_grads.wait()
    grads_part[...] = dot(part_v[...], grads_v[...]).astype(jnp.bfloat16)

    @pl.when(s != 0)
    def _():
        for copy in grads_in:
            copy.start()

    l_labels.wait()
    row_n, col_n = labels_v.shape
    cell = lax.broadcasted_iota(jnp.int32, (col_n, 128), 0) - j * LON_CELLS
    cell = jnp.where(cell < 0, cell + col_n, cell)
    pick_col = (cell == lax.broadcasted_iota(jnp.int32, (col_n, 128), 1)).astype(jnp.float32)
    row = lax.broadcasted_iota(jnp.int32, (row_n, row_n), 1) - i * LAT_CELLS
    row = jnp.where(row < 0, row + row_n, row)
    pick_row = (row == lax.broadcasted_iota(jnp.int32, (row_n, row_n), 0)).astype(jnp.float32)
    near_labels = dot(pick_row, dot(labels_v[...].astype(jnp.float32), pick_col))
    token_label = jnp.sum(dot(picks(5, TOKENS, row_n), near_labels) * picks(6, TOKENS, 128), -1, keepdims=True)
    lane = lax.broadcasted_iota(jnp.int32, (TOKENS, 128), 1).astype(jnp.float32)
    one_hot = (token_label == lane).astype(jnp.float32).astype(jnp.bfloat16)
    for w in range(2):
        here = one_hot[w * WIN:(w + 1) * WIN]
        alike = dot(here, jnp.concatenate([here] * HEADS, 0), NT)
        mask_v[w] = jnp.where(alike > 0.5, open_score, masked_score)

    per = D // (2 * nx * ny * nz)
    m = lax.broadcasted_iota(jnp.int32, (D, D), 0)
    r_at = m % per
    z_at = (m // per) % nz
    y_at = (m // (per * nz)) % ny
    x_at = (m // (per * nz * ny)) % nx
    c_at = m // (per * nz * ny * nx)
    feature = (
        (((x_at + x) % nx * ny + (y_at + y) % ny) * nz + (z_at + z) % nz) * 2 + (c_at + core) % 2
    ) * per + r_at
    perm_v[...] = (feature == lax.broadcasted_iota(jnp.int32, (D, D), 1)).astype(jnp.float32).astype(jnp.bfloat16)

    awin_v[...] = picks(2, TOKENS, ACTS_ROWS).astype(jnp.bfloat16)
    gwin_v[...] = picks(3, TOKENS, PART_ROWS).astype(jnp.bfloat16)
    back_v[...] = picks(1, PART_ROWS, TOKENS).astype(jnp.bfloat16)
    home_v[...] = picks(4, TOKENS, PART_ROWS).astype(jnp.bfloat16)
    pieces = ny * nz
    m = lax.broadcasted_iota(jnp.int32, regroup_v.shape, 0)
    old = (m // per) % 4 * (pieces * per) + m // (4 * per) * per + m % per
    regroup_v[...] = (old == lax.broadcasted_iota(jnp.int32, regroup_v.shape, 1)).astype(jnp.float32).astype(jnp.bfloat16)

    l_gain.wait()
    l_wqkv.wait()
    for copy in acts_in:
        copy.wait_recv()
    gain = gain_v[...]
    inputs = dot(awin_v[...], acts_buf[...])
    mean = jnp.mean(inputs, -1, keepdims=True)
    centred = inputs - mean
    inverse = 1.0 / jnp.sqrt(jnp.mean(centred * centred, -1, keepdims=True) + epsilon)
    centred = centred * inverse
    cen_v[...] = centred
    inv_v[...] = jnp.broadcast_to(inverse, inv_v.shape)
    projected = dot((centred * gain).astype(jnp.bfloat16), wqkv_v[...])
    for part in range(3):
        for w in range(2):
            for g in range(2):
                at = part * D + g * GROUP
                qkv_v[part, w * 2 + g] = projected[w * WIN:(w + 1) * WIN, at:at + GROUP].astype(jnp.bfloat16)

    head_lane = lax.broadcasted_iota(jnp.int32, (1, GROUP), 1) // 64
    head_mask = [(head_lane == h).astype(jnp.float32) for h in range(HEADS)]

    def spread(block, dst, n, scale):
        for h in range(HEADS):
            dst[n, h * WIN:(h + 1) * WIN, :] = (block * (head_mask[h] * scale)).astype(jnp.bfloat16)

    def gather(product):
        total = product[0:WIN] * head_mask[0]
        for h in range(1, HEADS):
            total = total + product[h * WIN:(h + 1) * WIN] * head_mask[h]
        return total

    def forward(n, carry):
        spread(qkv_v[0, n].astype(jnp.float32), qb_v, n, 0.125)
        scores = jnp.minimum(dot(qkv_v[1, n], qb_v[n], NT), mask_v[n // 2])
        exps = jnp.exp(scores - jnp.max(scores, 0, keepdims=True))
        weights = exps * (1.0 / jnp.sum(exps, 0, keepdims=True))
        w_v[n] = weights
        low = weights.astype(jnp.bfloat16)
        wl_v[n] = low
        att_v[n] = gather(dot(low, qkv_v[2, n], TN)).astype(jnp.bfloat16)
        return carry

    @pl.when(s == 0)
    def _():
        pl.semaphore_wait(ready_sem, 4)
        for copy in grads_in:
            copy.start()

    lax.fori_loop(0, 4, forward, 0, unroll=True)

    attended = jnp.concatenate(
        [jnp.concatenate([att_v[2 * w], att_v[2 * w + 1]], 1) for w in range(2)], 0
    )
    attended = dot(back_v[...], attended).astype(jnp.bfloat16)
    turned = dot(perm_v[...], attended, NT).astype(jnp.bfloat16)
    half = D // 2
    for copy in grads_in:
        copy.wait_recv()
    arrived = grads_buf[...]
    a_send[...] = dot(turned[half:], arrived).astype(jnp.bfloat16)
    step_a = send(a_send, a_recv, twin)
    own_v[...] = dot(turned[:half], arrived)

    upstream = dot(gwin_v[...], arrived).astype(jnp.bfloat16)
    up_v[...] = upstream
    l_wout.wait()
    grad_att = dot(upstream, wout_v[...], NT)
    for w in range(2):
        for g in range(2):
            ga_v[w * 2 + g] = grad_att[w * WIN:(w + 1) * WIN, g * GROUP:(g + 1) * GROUP].astype(jnp.bfloat16)

    def backward(n, carry):
        spread(ga_v[n].astype(jnp.float32), gb_v, n, 1.0)
        grad_w = dot(qkv_v[2, n], gb_v[n], NT)
        weights = w_v[n]
        inner = jnp.sum(grad_w * weights, 0, keepdims=True)
        grad_s = (weights * (grad_w - inner)).astype(jnp.bfloat16)
        gp_v[0, n] = (gather(dot(grad_s, qkv_v[1, n], TN)) * 0.125).astype(jnp.bfloat16)
        gp_v[1, n] = dot(grad_s, qb_v[n]).astype(jnp.bfloat16)
        gp_v[2, n] = dot(wl_v[n], gb_v[n]).astype(jnp.bfloat16)
        return carry

    lax.fori_loop(0, 2, backward, 0, unroll=True)

    step_a.wait_recv()
    chunk = half // nx
    summed = own_v[...] + a_recv[...].astype(jnp.float32)
    own_v[...] = summed
    b_send[...] = summed.astype(jnp.bfloat16)
    step_b = [
        send(b_send.at[pl.ds(k * chunk, chunk)], b_recv.at[pl.ds((k - 1) * chunk, chunk)], on_x(k))
        for k in range(1, nx)
    ]

    lax.fori_loop(2, 4, backward, 0, unroll=True)

    grad_proj = jnp.concatenate(
        [
            jnp.concatenate([gp_v[part, 2 * w + g] for part in range(3) for g in range(2)], 1)
            for w in range(2)
        ],
        0,
    )
    scaled = dot(grad_proj, wqkv_v[...], NT) * gain
    centred = cen_v[...]
    first = jnp.mean(scaled, -1, keepdims=True)
    second = jnp.mean(scaled * centred, -1, keepdims=True)
    branch = inv_v[:, 0:1] * (scaled - first - centred * second)
    result = (up_v[...].astype(jnp.float32) + branch).astype(jnp.bfloat16)
    for copy in step_b:
        copy.wait_recv()
    total = own_v[0:chunk, :]
    for k in range(1, nx):
        total = total + b_recv[(k - 1) * chunk:k * chunk, :].astype(jnp.float32)
    own_v[0:chunk, :] = total
    low = total.astype(jnp.bfloat16)
    stacked = jnp.concatenate([low[:, q * 128:(q + 1) * 128] for q in range(4)], 0)
    c_send[...] = dot(regroup_v[...], stacked).astype(jnp.bfloat16)
    size = 4 * per

    @pl.when(z == 0)
    def _():
        pl.semaphore_wait(across_sem, ny)

    step_c = [
        send(block(c_send, k * size, size), block(c_recv, k * size, size), on_yz(k))
        for k in sorted(range(1, pieces), key=lambda k: -min(k // nz, ny - k // nz) - 4 * (k % nz))
    ]

    back = dot(back_v[...], result).astype(jnp.bfloat16)
    ret_send[...] = back
    ret_recv[0:112, :] = back[0:112]
    ret_in = [
        send(block(ret_send, PART_AT[g], SIZE[g]), block(ret_recv, PART_AT[g], SIZE[g]), device)
        for g, device in (("10", near(0, 0, 1)), ("11", near(0, 1, 1)), ("01", near(0, 1, 0)))
    ]

    for copy in step_c:
        copy.wait_recv()
    got = c_recv[size:2 * size].astype(jnp.float32)
    for k in range(2, pieces):
        got = got + c_recv[k * size:(k + 1) * size].astype(jnp.float32)
    wo_ref[...] = own_v[0:per, :] + jnp.concatenate([got[q * per:(q + 1) * per] for q in range(4)], 1)

    for copy in ret_in:
        copy.wait_recv()
    out_ref[...] = dot(home_v[...], ret_recv[...]).astype(jnp.bfloat16)
    for copy in planned:
        copy.wait_send()


def on_device(sizes, acts, section_grads, gain, w_qkv, w_out, labels):
    pipe_n, nx, ny, nz = sizes
    per = D // (2 * nx * ny * nz)
    half = D // 2
    chunk = half // nx
    bf, f32 = jnp.bfloat16, jnp.float32
    table = layouts()
    sends = 3 + 4 + 3 + 1 + (nx - 1) + (ny * nz - 1)
    vm = pltpu.VMEM
    scratch = [
        vm((ACTS_ROWS, D), bf), vm((TOKENS, D), bf), vm((1, D), f32), vm((D, 3 * D), bf), vm((D, D), bf),
        vm(labels.shape, jnp.int32),
    ]
    scratch += [
        vm(table.shape, jnp.int32), vm((PART_ROWS, TOKENS), bf), vm((TOKENS, ACTS_ROWS), bf), vm((TOKENS, PART_ROWS), bf),
        vm((PART_ROWS, TOKENS), bf), vm((TOKENS, PART_ROWS), bf), vm((4 * chunk, 4 * chunk), bf),
    ]
    scratch += [
        vm((PART_ROWS - 112, D), bf), vm((PART_ROWS, D), bf), vm((PART_ROWS, D), bf), vm((PART_ROWS, D), bf), vm((PART_ROWS, D), bf),
    ]
    scratch += [
        vm((2, WIN, COLS), f32), vm((D, D), bf), vm((3, 4, WIN, GROUP), bf), vm((4, COLS, GROUP), bf),
        vm((4, WIN, COLS), f32), vm((4, WIN, COLS), bf), vm((4, WIN, GROUP), bf), vm((TOKENS, D), bf),
        vm((4, WIN, GROUP), bf), vm((4, COLS, GROUP), bf), vm((3, 4, WIN, GROUP), bf),
        vm((TOKENS, D), f32), vm((TOKENS, 128), f32),
    ]
    scratch += [
        vm((half, D), f32), vm((half, D), bf), vm((half, D), bf), vm((half, D), bf),
        vm((max(nx - 1, 1) * chunk, D), bf), vm((4 * chunk, 128), bf), vm((4 * chunk, 128), bf),
        pltpu.SemaphoreType.DMA((7,)),
        pltpu.SemaphoreType.DMA((sends,)), pltpu.SemaphoreType.DMA((sends,)), pltpu.SemaphoreType.REGULAR,
        pltpu.SemaphoreType.REGULAR,
    ]
    anywhere = pl.BlockSpec(memory_space=pltpu.HBM)
    out, wo = pl.pallas_call(
        functools.partial(kernel, sizes),
        out_shape=(pltpu.VMEM((TOKENS, D), bf), pltpu.VMEM((per, D), f32)),
        in_specs=[anywhere] * 7,
        out_specs=(pl.BlockSpec(memory_space=pltpu.VMEM), pl.BlockSpec(memory_space=pltpu.VMEM)),
        scratch_shapes=scratch,
        compiler_params=pltpu.CompilerParams(
            collective_id=0, has_side_effects=True, vmem_limit_bytes=60 * 1024 * 1024
        ),
        name="sublayer",
    )(
        acts.reshape(TOKENS, D), section_grads.reshape(TOKENS, D), gain, w_qkv[0], w_out[0], labels,
        jnp.asarray(table),
    )
    return out.reshape(acts.shape), wo


def solution(mesh):
    pipe_n, lon_n, lat_n = (mesh.shape[axis] for axis in ("pipe", "lon", "lat"))
    ny = 8 if lon_n == 32 else min(lon_n, 2)
    sizes = (pipe_n, lon_n // ny, ny, lat_n // 2)
    in_specs = (
        P("pipe", None, "lat", "lon", None),
        P("pipe", None, "lat", "lon", None),
        P("pipe", None),
        P("pipe", None, None),
        P("pipe", None, None),
        P(),
    )
    out_specs = (P("pipe", None, "lat", "lon", None), P(("pipe", "lon", "lat"), None))
    return jax.shard_map(
        functools.partial(on_device, sizes), mesh=mesh, in_specs=in_specs, out_specs=out_specs, check_vma=False
    )
```

```python
import functools

import jax
import jax.numpy as jnp
import numpy as np
from jax import lax
from jax.experimental import pallas as pl
from jax.experimental.pallas import tpu as pltpu
from jax.sharding import PartitionSpec as P

MESH = pl.DeviceIdType.MESH
LEV = 2
LAT_CELLS = 6
LON_CELLS = 24
TOKENS = 288
WIN = 144
D = 512
GROUP = 256
HEADS = 4
COLS = HEADS * WIN
PART_AT = {"00": 0, "10": 112, "01": 224, "11": 272}
PART_ROWS = 320
ACTS_AT = {"own": 0, "10": 288, "01": 400, "11": 448}
ACTS_ROWS = 496
SIZE = {"00": 112, "10": 112, "01": 48, "11": 48}
epsilon = 1e-05
masked_score = -1e30
open_score = 3e38


def natural(lev, row, col):
    return (lev * LAT_CELLS + row) * LON_CELLS + col


def cells(group, part):
    rows = range(0, 3) if group[0] == "1" else range(3, 6)
    if group[1] == "1":
        cols = range(0, 6) if part == 1 else ()
    else:
        cols = range(6, 18) if part == 0 else range(18, 24)
    return [(l, r, c) for l in range(LEV) for r in rows for c in cols]


def layouts():
    groups = ("00", "10", "01", "11")
    place = {g: {cell: n for n, cell in enumerate(cells(g, 0) + cells(g, 1))} for g in groups}

    table = np.full((PART_ROWS, 8), -1, np.int32)
    order = [(g, cell) for w in range(2) for g in groups for cell in cells(g, w)]
    for t, (g, cell) in enumerate(order):
        n = place[g][cell]
        table[PART_AT[g] + n, 0] = natural(*cell)
        table[PART_AT[g] + n, 1] = t
        table[t, 2] = natural(*cell) if g == "00" else ACTS_AT[g] + n
        table[t, 3] = PART_AT[g] + n
        table[natural(*cell), 4] = PART_AT[g] + n
        table[t, 5] = cell[1] + (6 if g[0] == "1" else 0)
        table[t, 6] = cell[2] + (24 if g[1] == "1" else 0)
    return table


def dot(left, right, dims=((1,), (0,))):
    return lax.dot_general(left, right, (dims, ((), ())), preferred_element_type=jnp.float32)


NT = ((1,), (1,))
TN = ((0,), (0,))


def kernel(
    sizes,
    acts_hbm, grads_hbm, gain_hbm, wqkv_hbm, wout_hbm, labels_hbm,
    table_hbm,
    out_ref, wo_ref,
    acts_buf, grads_v, gain_v, wqkv_v, wout_v, labels_v,
    table_v,
    part_v, awin_v, gwin_v, back_v, home_v, regroup_v,
    acts_part, grads_part, grads_buf, ret_send, ret_recv,
    mask_v, perm_v, qkv_v, qb_v, w_v, wl_v, att_v, up_v, ga_v, gb_v, gp_v, cen_v, inv_v,
    own_v, a_send, a_recv, b_send, b_recv, c_send, c_recv,
    in_sem, send_sem, recv_sem, ready_sem, across_sem,
):
    pipe_n, nx, ny, nz = sizes
    lon_n, lat_n = nx * ny, nz * 2
    s = lax.axis_index("pipe")
    j = lax.axis_index("lon")
    i = lax.axis_index("lat")
    x, y = j // ny, j % ny
    z, core = i // 2, i % 2

    def near(ds, dj, di):
        return (
            (s + ds + pipe_n) % pipe_n if ds else s,
            (j + dj + lon_n) % lon_n if dj else j,
            (i + di + lat_n) % lat_n if di else i,
        )

    def on_x(k):
        return (s, ((x + k) % nx) * ny + y, i)

    def on_yz(k):
        return (s, x * ny + (y + k // nz) % ny, (z + k % nz) % nz * 2 + core)

    twin = (s, j, z * 2 + (1 - core))

    loads = []
    for n, (src, dst) in enumerate((
        (table_hbm, table_v), (acts_hbm, acts_buf.at[pl.ds(0, TOKENS)]), (grads_hbm, grads_v), (labels_hbm, labels_v),
        (gain_hbm, gain_v), (wqkv_hbm, wqkv_v), (wout_hbm, wout_v),
    )):
        load = pltpu.make_async_copy(src, dst, in_sem.at[n])
        load.start()
        loads.append(load)
    l_table, l_acts, l_grads, l_labels, l_gain, l_wqkv, l_wout = loads

    barrier = pltpu.get_barrier_semaphore()
    greeted = [near(0, 0, 1), near(0, 1, 1), near(0, 0, -1), near(0, -1, -1), near(0, 1, 0), near(0, -1, 0), twin]
    greeted += [on_x(k) for k in range(1, nx)] + [on_yz(k * nz) for k in range(1, ny)]
    across = [on_yz(k * nz + 1) for k in range(ny)]
    before = [near(-1, 0, 0), near(-1, 0, -1), near(-1, -1, 0), near(-1, -1, -1)]
    after = [near(1, 0, 0), near(1, 0, 1), near(1, 1, 0), near(1, 1, 1)]
    last = pipe_n - 1

    def greet(devices):
        for device in devices:
            pl.semaphore_signal(barrier, inc=1, device_id=device, device_id_type=MESH)

    greet(greeted)

    @pl.when(s != last)
    def _():
        greet(after)

    @pl.when(s == 0)
    def _():
        greet(before)

    @pl.when(z == 0)
    def _():
        greet(across)


    def picks(column, rows, cols):
        found = table_v[0:rows, column:column + 1] == lax.broadcasted_iota(jnp.int32, (rows, cols), 1)
        return found.astype(jnp.float32)

    planned = []

    def plan(src, dst, device):
        n = len(planned)
        copy = pltpu.make_async_remote_copy(
            src_ref=src, dst_ref=dst, send_sem=send_sem.at[n], recv_sem=recv_sem.at[n],
            device_id=device, device_id_type=MESH,
        )
        planned.append(copy)
        return copy

    def send(src, dst, device):
        copy = plan(src, dst, device)
        copy.start()
        return copy

    def block(ref, at, size):
        return ref.at[pl.ds(at, size)]

    here = {"10": (0, -1), "11": (-1, -1), "00": (0, 0), "01": (-1, 0)}
    acts_in = [
        plan(block(acts_part, PART_AT[g] - 112, SIZE[g]), block(acts_buf, ACTS_AT[g], SIZE[g]), near(0, *here[g]))
        for g in ("10", "11", "01")
    ]
    grads_in = [
        plan(block(grads_part, PART_AT[g], SIZE[g]), block(grads_buf, PART_AT[g], SIZE[g]), near(-1, *here[g]))
        for g in ("10", "11", "00", "01")
    ]

    l_table.wait()
    part_v[...] = picks(0, PART_ROWS, TOKENS).astype(jnp.bfloat16)
    l_acts.wait()
    acts_part[...] = dot(part_v[112:], acts_buf[0:TOKENS]).astype(jnp.bfloat16)
    l_grads.wait()
    grads_part[...] = dot(part_v[...], grads_v[...]).astype(jnp.bfloat16)
    pl.semaphore_wait(barrier, len(greeted) + jnp.where(s > 0, 4, 0) + jnp.where(s == last, 4, 0) + jnp.where(z > 0, ny, 0))

    @pl.when(s == last)
    def _():
        for device in after:
            pl.semaphore_signal(ready_sem, inc=1, device_id=device, device_id_type=MESH)

    @pl.when(z > 0)
    def _():
        for device in across:
            pl.semaphore_signal(across_sem, inc=1, device_id=device, device_id_type=MESH)

    for copy in acts_in:
        copy.start()

    @pl.when(s != 0)
    def _():
        for copy in grads_in:
            copy.start()

    l_labels.wait()
    row_n, col_n = labels_v.shape
    cell = lax.broadcasted_iota(jnp.int32, (col_n, 128), 0) - j * LON_CELLS
    cell = jnp.where(cell < 0, cell + col_n, cell)
    pick_col = (cell == lax.broadcasted_iota(jnp.int32, (col_n, 128), 1)).astype(jnp.float32)
    row = lax.broadcasted_iota(jnp.int32, (row_n, row_n), 1) - i * LAT_CELLS
    row = jnp.where(row < 0, row + row_n, row)
    pick_row = (row == lax.broadcasted_iota(jnp.int32, (row_n, row_n), 0)).astype(jnp.float32)
    near_labels = dot(pick_row, dot(labels_v[...].astype(jnp.float32), pick_col))
    token_label = jnp.sum(dot(picks(5, TOKENS, row_n), near_labels) * picks(6, TOKENS, 128), -1, keepdims=True)
    lane = lax.broadcasted_iota(jnp.int32, (TOKENS, 128), 1).astype(jnp.float32)
    one_hot = (token_label == lane).astype(jnp.float32).astype(jnp.bfloat16)
    for w in range(2):
        here = one_hot[w * WIN:(w + 1) * WIN]
        alike = dot(here, jnp.concatenate([here] * HEADS, 0), NT)
        mask_v[w] = jnp.where(alike > 0.5, open_score, masked_score)

    per = D // (2 * nx * ny * nz)
    m = lax.broadcasted_iota(jnp.int32, (D, D), 0)
    r_at = m % per
    z_at = (m // per) % nz
    y_at = (m // (per * nz)) % ny
    x_at = (m // (per * nz * ny)) % nx
    c_at = m // (per * nz * ny * nx)
    feature = (
        (((x_at + x) % nx * ny + (y_at + y) % ny) * nz + (z_at + z) % nz) * 2 + (c_at + core) % 2
    ) * per + r_at
    perm_v[...] = (feature == lax.broadcasted_iota(jnp.int32, (D, D), 1)).astype(jnp.float32).astype(jnp.bfloat16)

    awin_v[...] = picks(2, TOKENS, ACTS_ROWS).astype(jnp.bfloat16)
    gwin_v[...] = picks(3, TOKENS, PART_ROWS).astype(jnp.bfloat16)
    back_v[...] = picks(1, PART_ROWS, TOKENS).astype(jnp.bfloat16)
    home_v[...] = picks(4, TOKENS, PART_ROWS).astype(jnp.bfloat16)
    pieces = ny * nz
    m = lax.broadcasted_iota(jnp.int32, regroup_v.shape, 0)
    old = (m // per) % 4 * (pieces * per) + m // (4 * per) * per + m % per
    regroup_v[...] = (old == lax.broadcasted_iota(jnp.int32, regroup_v.shape, 1)).astype(jnp.float32).astype(jnp.bfloat16)

    l_gain.wait()
    l_wqkv.wait()
    for copy in acts_in:
        copy.wait_recv()
    gain = gain_v[...]
    inputs = dot(awin_v[...], acts_buf[...])
    mean = jnp.mean(inputs, -1, keepdims=True)
    centred = inputs - mean
    inverse = 1.0 / jnp.sqrt(jnp.mean(centred * centred, -1, keepdims=True) + epsilon)
    centred = centred * inverse
    cen_v[...] = centred
    inv_v[...] = jnp.broadcast_to(inverse, inv_v.shape)
    projected = dot((centred * gain).astype(jnp.bfloat16), wqkv_v[...])
    for part in range(3):
        for w in range(2):
            for g in range(2):
                at = part * D + g * GROUP
                qkv_v[part, w * 2 + g] = projected[w * WIN:(w + 1) * WIN, at:at + GROUP].astype(jnp.bfloat16)

    head_lane = lax.broadcasted_iota(jnp.int32, (1, GROUP), 1) // 64
    head_mask = [(head_lane == h).astype(jnp.float32) for h in range(HEADS)]

    def spread(block, dst, n, scale):
        for h in range(HEADS):
            dst[n, h * WIN:(h + 1) * WIN, :] = (block * (head_mask[h] * scale)).astype(jnp.bfloat16)

    def gather(product):
        total = product[0:WIN] * head_mask[0]
        for h in range(1, HEADS):
            total = total + product[h * WIN:(h + 1) * WIN] * head_mask[h]
        return total

    def forward(n, carry):
        spread(qkv_v[0, n].astype(jnp.float32), qb_v, n, 0.125)
        scores = jnp.minimum(dot(qkv_v[1, n], qb_v[n], NT), mask_v[n // 2])
        exps = jnp.exp(scores - jnp.max(scores, 0, keepdims=True))
        weights = exps * (1.0 / jnp.sum(exps, 0, keepdims=True))
        w_v[n] = weights
        low = weights.astype(jnp.bfloat16)
        wl_v[n] = low
        att_v[n] = gather(dot(low, qkv_v[2, n], TN)).astype(jnp.bfloat16)
        return carry

    @pl.when(s == 0)
    def _():
        pl.semaphore_wait(ready_sem, 4)
        for copy in grads_in:
            copy.start()

    lax.fori_loop(0, 4, forward, 0, unroll=True)

    attended = jnp.concatenate(
        [jnp.concatenate([att_v[2 * w], att_v[2 * w + 1]], 1) for w in range(2)], 0
    )
    attended = dot(back_v[...], attended).astype(jnp.bfloat16)
    turned = dot(perm_v[...], attended, NT).astype(jnp.bfloat16)
    half = D // 2
    for copy in grads_in:
        copy.wait_recv()
    arrived = grads_buf[...]
    a_send[...] = dot(turned[half:], arrived).astype(jnp.bfloat16)
    step_a = send(a_send, a_recv, twin)
    own_v[...] = dot(turned[:half], arrived)

    upstream = dot(gwin_v[...], arrived).astype(jnp.bfloat16)
    up_v[...] = upstream
    l_wout.wait()
    grad_att = dot(upstream, wout_v[...], NT)
    for w in range(2):
        for g in range(2):
            ga_v[w * 2 + g] = grad_att[w * WIN:(w + 1) * WIN, g * GROUP:(g + 1) * GROUP].astype(jnp.bfloat16)

    def backward(n, carry):
        spread(ga_v[n].astype(jnp.float32), gb_v, n, 1.0)
        grad_w = dot(qkv_v[2, n], gb_v[n], NT)
        weights = w_v[n]
        inner = jnp.sum(grad_w * weights, 0, keepdims=True)
        grad_s = (weights * (grad_w - inner)).astype(jnp.bfloat16)
        gp_v[0, n] = (gather(dot(grad_s, qkv_v[1, n], TN)) * 0.125).astype(jnp.bfloat16)
        gp_v[1, n] = dot(grad_s, qb_v[n]).astype(jnp.bfloat16)
        gp_v[2, n] = dot(wl_v[n], gb_v[n]).astype(jnp.bfloat16)
        return carry

    lax.fori_loop(0, 1, backward, 0, unroll=True)

    step_a.wait_recv()
    chunk = half // nx
    summed = own_v[...] + a_recv[...].astype(jnp.float32)
    own_v[...] = summed
    b_send[...] = summed.astype(jnp.bfloat16)
    step_b = [
        send(b_send.at[pl.ds(k * chunk, chunk)], b_recv.at[pl.ds((k - 1) * chunk, chunk)], on_x(k))
        for k in sorted(range(1, nx), key=lambda k: -min(k, nx - k))
    ]

    lax.fori_loop(1, 4, backward, 0, unroll=True)

    grad_proj = jnp.concatenate(
        [
            jnp.concatenate([gp_v[part, 2 * w + g] for part in range(3) for g in range(2)], 1)
            for w in range(2)
        ],
        0,
    )
    scaled = dot(grad_proj, wqkv_v[...], NT) * gain
    centred = cen_v[...]
    first = jnp.mean(scaled, -1, keepdims=True)
    second = jnp.mean(scaled * centred, -1, keepdims=True)
    branch = inv_v[:, 0:1] * (scaled - first - centred * second)
    result = (up_v[...].astype(jnp.float32) + branch).astype(jnp.bfloat16)
    back = dot(back_v[...], result).astype(jnp.bfloat16)
    ret_send[...] = back
    ret_recv[0:112, :] = back[0:112]
    ret_in = [
        send(block(ret_send, PART_AT[g], SIZE[g]), block(ret_recv, PART_AT[g], SIZE[g]), device)
        for g, device in (("10", near(0, 0, 1)), ("11", near(0, 1, 1)), ("01", near(0, 1, 0)))
    ]

    for copy in step_b:
        copy.wait_recv()
    total = own_v[0:chunk, :]
    for k in range(1, nx):
        total = total + b_recv[(k - 1) * chunk:k * chunk, :].astype(jnp.float32)
    own_v[0:chunk, :] = total
    low = total.astype(jnp.bfloat16)
    stacked = jnp.concatenate([low[:, q * 128:(q + 1) * 128] for q in range(4)], 0)
    c_send[...] = dot(regroup_v[...], stacked).astype(jnp.bfloat16)
    size = 4 * per

    @pl.when(z == 0)
    def _():
        pl.semaphore_wait(across_sem, ny)

    step_c = [
        send(block(c_send, k * size, size), block(c_recv, k * size, size), on_yz(k))
        for k in sorted(range(1, pieces), key=lambda k: -min(k // nz, ny - k // nz) - 4 * (k % nz))
    ]

    for copy in ret_in:
        copy.wait_recv()
    out_ref[...] = dot(home_v[...], ret_recv[...]).astype(jnp.bfloat16)
    for copy in step_c:
        copy.wait_recv()
    got = c_recv[size:2 * size].astype(jnp.float32)
    for k in range(2, pieces):
        got = got + c_recv[k * size:(k + 1) * size].astype(jnp.float32)
    wo_ref[...] = own_v[0:per, :] + jnp.concatenate([got[q * per:(q + 1) * per] for q in range(4)], 1)

    for copy in planned:
        copy.wait_send()


def on_device(sizes, acts, section_grads, gain, w_qkv, w_out, labels):
    pipe_n, nx, ny, nz = sizes
    per = D // (2 * nx * ny * nz)
    half = D // 2
    chunk = half // nx
    bf, f32 = jnp.bfloat16, jnp.float32
    table = layouts()
    sends = 3 + 4 + 3 + 1 + (nx - 1) + (ny * nz - 1)
    vm = pltpu.VMEM
    scratch = [
        vm((ACTS_ROWS, D), bf), vm((TOKENS, D), bf), vm((1, D), f32), vm((D, 3 * D), bf), vm((D, D), bf),
        vm(labels.shape, jnp.int32),
    ]
    scratch += [
        vm(table.shape, jnp.int32), vm((PART_ROWS, TOKENS), bf), vm((TOKENS, ACTS_ROWS), bf), vm((TOKENS, PART_ROWS), bf),
        vm((PART_ROWS, TOKENS), bf), vm((TOKENS, PART_ROWS), bf), vm((4 * chunk, 4 * chunk), bf),
    ]
    scratch += [
        vm((PART_ROWS - 112, D), bf), vm((PART_ROWS, D), bf), vm((PART_ROWS, D), bf), vm((PART_ROWS, D), bf), vm((PART_ROWS, D), bf),
    ]
    scratch += [
        vm((2, WIN, COLS), f32), vm((D, D), bf), vm((3, 4, WIN, GROUP), bf), vm((4, COLS, GROUP), bf),
        vm((4, WIN, COLS), f32), vm((4, WIN, COLS), bf), vm((4, WIN, GROUP), bf), vm((TOKENS, D), bf),
        vm((4, WIN, GROUP), bf), vm((4, COLS, GROUP), bf), vm((3, 4, WIN, GROUP), bf),
        vm((TOKENS, D), f32), vm((TOKENS, 128), f32),
    ]
    scratch += [
        vm((half, D), f32), vm((half, D), bf), vm((half, D), bf), vm((half, D), bf),
        vm((max(nx - 1, 1) * chunk, D), bf), vm((4 * chunk, 128), bf), vm((4 * chunk, 128), bf),
        pltpu.SemaphoreType.DMA((7,)),
        pltpu.SemaphoreType.DMA((sends,)), pltpu.SemaphoreType.DMA((sends,)), pltpu.SemaphoreType.REGULAR,
        pltpu.SemaphoreType.REGULAR,
    ]
    anywhere = pl.BlockSpec(memory_space=pltpu.HBM)
    out, wo = pl.pallas_call(
        functools.partial(kernel, sizes),
        out_shape=(pltpu.VMEM((TOKENS, D), bf), pltpu.VMEM((per, D), f32)),
        in_specs=[anywhere] * 7,
        out_specs=(pl.BlockSpec(memory_space=pltpu.VMEM), pl.BlockSpec(memory_space=pltpu.VMEM)),
        scratch_shapes=scratch,
        compiler_params=pltpu.CompilerParams(
            collective_id=0, has_side_effects=True, vmem_limit_bytes=60 * 1024 * 1024
        ),
        name="sublayer",
    )(
        acts.reshape(TOKENS, D), section_grads.reshape(TOKENS, D), gain, w_qkv[0], w_out[0], labels,
        jnp.asarray(table),
    )
    return out.reshape(acts.shape), wo


def solution(mesh):
    pipe_n, lon_n, lat_n = (mesh.shape[axis] for axis in ("pipe", "lon", "lat"))
    ny = 8 if lon_n == 32 else min(lon_n, 2)
    sizes = (pipe_n, lon_n // ny, ny, lat_n // 2)
    in_specs = (
        P("pipe", None, "lat", "lon", None),
        P("pipe", None, "lat", "lon", None),
        P("pipe", None),
        P("pipe", None, None),
        P("pipe", None, None),
        P(),
    )
    out_specs = (P("pipe", None, "lat", "lon", None), P(("pipe", "lon", "lat"), None))
    return jax.shard_map(
        functools.partial(on_device, sizes), mesh=mesh, in_specs=in_specs, out_specs=out_specs, check_vma=False
    )
```

```python
import functools

import jax
import jax.numpy as jnp
import numpy as np
from jax import lax
from jax.experimental import pallas as pl
from jax.experimental.pallas import tpu as pltpu
from jax.sharding import PartitionSpec as P

MESH = pl.DeviceIdType.MESH
LEV = 2
LAT_CELLS = 6
LON_CELLS = 24
TOKENS = 288
WIN = 144
D = 512
GROUP = 256
HEADS = 4
COLS = HEADS * WIN
PART_AT = {"00": 0, "10": 112, "01": 224, "11": 272}
PART_ROWS = 320
ACTS_AT = {"own": 0, "10": 288, "01": 400, "11": 448}
ACTS_ROWS = 496
SIZE = {"00": 112, "10": 112, "01": 48, "11": 48}
epsilon = 1e-05
masked_score = -1e30
open_score = 3e38


def natural(lev, row, col):
    return (lev * LAT_CELLS + row) * LON_CELLS + col


def cells(group, part):
    rows = range(0, 3) if group[0] == "1" else range(3, 6)
    if group[1] == "1":
        cols = range(0, 6) if part == 1 else ()
    else:
        cols = range(6, 18) if part == 0 else range(18, 24)
    return [(l, r, c) for l in range(LEV) for r in rows for c in cols]


def layouts():
    groups = ("00", "10", "01", "11")
    place = {g: {cell: n for n, cell in enumerate(cells(g, 0) + cells(g, 1))} for g in groups}

    table = np.full((PART_ROWS, 8), -1, np.int32)
    order = [(g, cell) for w in range(2) for g in groups for cell in cells(g, w)]
    for t, (g, cell) in enumerate(order):
        n = place[g][cell]
        table[PART_AT[g] + n, 0] = natural(*cell)
        table[PART_AT[g] + n, 1] = t
        table[t, 2] = natural(*cell) if g == "00" else ACTS_AT[g] + n
        table[t, 3] = PART_AT[g] + n
        table[natural(*cell), 4] = PART_AT[g] + n
        table[t, 5] = cell[1] + (6 if g[0] == "1" else 0)
        table[t, 6] = cell[2] + (24 if g[1] == "1" else 0)
    return table


def dot(left, right, dims=((1,), (0,))):
    return lax.dot_general(left, right, (dims, ((), ())), preferred_element_type=jnp.float32)


NT = ((1,), (1,))
TN = ((0,), (0,))


def kernel(
    sizes,
    acts_hbm, grads_hbm, gain_hbm, wqkv_hbm, wout_hbm, labels_hbm,
    table_hbm,
    out_ref, wo_ref,
    acts_buf, grads_v, gain_v, wqkv_v, wout_v, labels_v,
    table_v,
    part_v, awin_v, gwin_v, back_v, home_v, regroup_v,
    acts_part, grads_part, grads_buf, ret_send, ret_recv,
    mask_v, perm_v, qkv_v, qb_v, w_v, wl_v, att_v, up_v, ga_v, gb_v, gp_v, cen_v, inv_v,
    own_v, a_send, a_recv, b_send, b_recv, c_send, c_recv,
    in_sem, send_sem, recv_sem, ready_sem, across_sem,
):
    pipe_n, nx, ny, nz = sizes
    lon_n, lat_n = nx * ny, nz * 2
    s = lax.axis_index("pipe")
    j = lax.axis_index("lon")
    i = lax.axis_index("lat")
    x, y = j // ny, j % ny
    z, core = i // 2, i % 2

    def near(ds, dj, di):
        return (
            (s + ds + pipe_n) % pipe_n if ds else s,
            (j + dj + lon_n) % lon_n if dj else j,
            (i + di + lat_n) % lat_n if di else i,
        )

    def on_x(k):
        return (s, ((x + k) % nx) * ny + y, i)

    def on_yz(k):
        return (s, x * ny + (y + k // nz) % ny, (z + k % nz) % nz * 2 + core)

    twin = (s, j, z * 2 + (1 - core))

    loads = []
    for n, (src, dst) in enumerate((
        (table_hbm, table_v), (acts_hbm, acts_buf.at[pl.ds(0, TOKENS)]), (grads_hbm, grads_v), (labels_hbm, labels_v),
        (gain_hbm, gain_v), (wqkv_hbm, wqkv_v), (wout_hbm, wout_v),
    )):
        load = pltpu.make_async_copy(src, dst, in_sem.at[n])
        load.start()
        loads.append(load)
    l_table, l_acts, l_grads, l_labels, l_gain, l_wqkv, l_wout = loads

    barrier = pltpu.get_barrier_semaphore()
    greeted = [near(0, 0, 1), near(0, 1, 1), near(0, 0, -1), near(0, -1, -1), near(0, 1, 0), near(0, -1, 0), twin]
    greeted += [on_x(k) for k in range(1, nx)] + [on_yz(k * nz) for k in range(1, ny)]
    across = [on_yz(k * nz + 1) for k in range(ny)]
    before = [near(-1, 0, 0), near(-1, 0, -1), near(-1, -1, 0), near(-1, -1, -1)]
    after = [near(1, 0, 0), near(1, 0, 1), near(1, 1, 0), near(1, 1, 1)]
    last = pipe_n - 1

    def greet(devices):
        for device in devices:
            pl.semaphore_signal(barrier, inc=1, device_id=device, device_id_type=MESH)

    greet(greeted)

    @pl.when(s != last)
    def _():
        greet(after)

    @pl.when(s == 0)
    def _():
        greet(before)

    @pl.when(z == 0)
    def _():
        greet(across)


    def picks(column, rows, cols):
        found = table_v[0:rows, column:column + 1] == lax.broadcasted_iota(jnp.int32, (rows, cols), 1)
        return found.astype(jnp.float32)

    planned = []

    def plan(src, dst, device):
        n = len(planned)
        copy = pltpu.make_async_remote_copy(
            src_ref=src, dst_ref=dst, send_sem=send_sem.at[n], recv_sem=recv_sem.at[n],
            device_id=device, device_id_type=MESH,
        )
        planned.append(copy)
        return copy

    def send(src, dst, device):
        copy = plan(src, dst, device)
        copy.start()
        return copy

    def block(ref, at, size):
        return ref.at[pl.ds(at, size)]

    here = {"10": (0, -1), "11": (-1, -1), "00": (0, 0), "01": (-1, 0)}
    acts_in = [
        plan(block(acts_part, PART_AT[g] - 112, SIZE[g]), block(acts_buf, ACTS_AT[g], SIZE[g]), near(0, *here[g]))
        for g in ("10", "11", "01")
    ]
    grads_in = [
        plan(block(grads_part, PART_AT[g], SIZE[g]), block(grads_buf, PART_AT[g], SIZE[g]), near(-1, *here[g]))
        for g in ("10", "11", "00", "01")
    ]

    l_table.wait()
    part_v[...] = picks(0, PART_ROWS, TOKENS).astype(jnp.bfloat16)
    l_acts.wait()
    acts_part[...] = dot(part_v[112:], acts_buf[0:TOKENS]).astype(jnp.bfloat16)
    l_grads.wait()
    grads_part[...] = dot(part_v[...], grads_v[...]).astype(jnp.bfloat16)
    pl.semaphore_wait(barrier, len(greeted) + jnp.where(s > 0, 4, 0) + jnp.where(s == last, 4, 0) + jnp.where(z > 0, ny, 0))

    @pl.when(s == last)
    def _():
        for device in after:
            pl.semaphore_signal(ready_sem, inc=1, device_id=device, device_id_type=MESH)

    @pl.when(z > 0)
    def _():
        for device in across:
            pl.semaphore_signal(across_sem, inc=1, device_id=device, device_id_type=MESH)

    for copy in acts_in:
        copy.start()

    @pl.when(s != 0)
    def _():
        for copy in grads_in:
            copy.start()

    l_labels.wait()
    row_n, col_n = labels_v.shape
    cell = lax.broadcasted_iota(jnp.int32, (col_n, 128), 0) - j * LON_CELLS
    cell = jnp.where(cell < 0, cell + col_n, cell)
    pick_col = (cell == lax.broadcasted_iota(jnp.int32, (col_n, 128), 1)).astype(jnp.float32)
    row = lax.broadcasted_iota(jnp.int32, (row_n, row_n), 1) - i * LAT_CELLS
    row = jnp.where(row < 0, row + row_n, row)
    pick_row = (row == lax.broadcasted_iota(jnp.int32, (row_n, row_n), 0)).astype(jnp.float32)
    near_labels = dot(pick_row, dot(labels_v[...].astype(jnp.float32), pick_col))
    token_label = jnp.sum(dot(picks(5, TOKENS, row_n), near_labels) * picks(6, TOKENS, 128), -1, keepdims=True)
    lane = lax.broadcasted_iota(jnp.int32, (TOKENS, 128), 1).astype(jnp.float32)
    one_hot = (token_label == lane).astype(jnp.float32).astype(jnp.bfloat16)
    for w in range(2):
        here = one_hot[w * WIN:(w + 1) * WIN]
        alike = dot(here, jnp.concatenate([here] * HEADS, 0), NT)
        mask_v[w] = jnp.where(alike > 0.5, open_score, masked_score)

    per = D // (2 * nx * ny * nz)
    m = lax.broadcasted_iota(jnp.int32, (D, D), 0)
    r_at = m % per
    z_at = (m // per) % nz
    y_at = (m // (per * nz)) % ny
    x_at = (m // (per * nz * ny)) % nx
    c_at = m // (per * nz * ny * nx)
    feature = (
        (((x_at + x) % nx * ny + (y_at + y) % ny) * nz + (z_at + z) % nz) * 2 + (c_at + core) % 2
    ) * per + r_at
    perm_v[...] = (feature == lax.broadcasted_iota(jnp.int32, (D, D), 1)).astype(jnp.float32).astype(jnp.bfloat16)

    awin_v[...] = picks(2, TOKENS, ACTS_ROWS).astype(jnp.bfloat16)
    gwin_v[...] = picks(3, TOKENS, PART_ROWS).astype(jnp.bfloat16)
    back_v[...] = picks(1, PART_ROWS, TOKENS).astype(jnp.bfloat16)
    home_v[...] = picks(4, TOKENS, PART_ROWS).astype(jnp.bfloat16)
    pieces = ny * nz
    m = lax.broadcasted_iota(jnp.int32, regroup_v.shape, 0)
    old = (m // per) % 4 * (pieces * per) + m // (4 * per) * per + m % per
    regroup_v[...] = (old == lax.broadcasted_iota(jnp.int32, regroup_v.shape, 1)).astype(jnp.float32).astype(jnp.bfloat16)

    @pl.when((s == 0) & (core == 1) & (z == 0))
    def _():
        pl.semaphore_wait(ready_sem, 4)
        for copy in grads_in:
            copy.start()

    l_gain.wait()
    l_wqkv.wait()
    for copy in acts_in:
        copy.wait_recv()
    gain = gain_v[...]
    inputs = dot(awin_v[...], acts_buf[...])
    mean = jnp.mean(inputs, -1, keepdims=True)
    centred = inputs - mean
    inverse = 1.0 / jnp.sqrt(jnp.mean(centred * centred, -1, keepdims=True) + epsilon)
    centred = centred * inverse
    cen_v[...] = centred
    inv_v[...] = jnp.broadcast_to(inverse, inv_v.shape)
    projected = dot((centred * gain).astype(jnp.bfloat16), wqkv_v[...])
    for part in range(3):
        for w in range(2):
            for g in range(2):
                at = part * D + g * GROUP
                qkv_v[part, w * 2 + g] = projected[w * WIN:(w + 1) * WIN, at:at + GROUP].astype(jnp.bfloat16)

    head_lane = lax.broadcasted_iota(jnp.int32, (1, GROUP), 1) // 64
    head_mask = [(head_lane == h).astype(jnp.float32) for h in range(HEADS)]

    def spread(block, dst, n, scale):
        for h in range(HEADS):
            dst[n, h * WIN:(h + 1) * WIN, :] = (block * (head_mask[h] * scale)).astype(jnp.bfloat16)

    def gather(product):
        total = product[0:WIN] * head_mask[0]
        for h in range(1, HEADS):
            total = total + product[h * WIN:(h + 1) * WIN] * head_mask[h]
        return total

    def forward(n, carry):
        spread(qkv_v[0, n].astype(jnp.float32), qb_v, n, 0.125)
        scores = jnp.minimum(dot(qkv_v[1, n], qb_v[n], NT), mask_v[n // 2])
        exps = jnp.exp(scores - jnp.max(scores, 0, keepdims=True))
        weights = exps * (1.0 / jnp.sum(exps, 0, keepdims=True))
        w_v[n] = weights
        low = weights.astype(jnp.bfloat16)
        wl_v[n] = low
        att_v[n] = gather(dot(low, qkv_v[2, n], TN)).astype(jnp.bfloat16)
        return carry

    @pl.when((s == 0) & ((core == 0) | (z > 0)))
    def _():
        pl.semaphore_wait(ready_sem, 4)
        for copy in grads_in:
            copy.start()

    lax.fori_loop(0, 4, forward, 0, unroll=True)

    attended = jnp.concatenate(
        [jnp.concatenate([att_v[2 * w], att_v[2 * w + 1]], 1) for w in range(2)], 0
    )
    attended = dot(back_v[...], attended).astype(jnp.bfloat16)
    turned = dot(perm_v[...], attended, NT).astype(jnp.bfloat16)
    half = D // 2
    for copy in grads_in:
        copy.wait_recv()
    arrived = grads_buf[...]
    a_send[...] = dot(turned[half:], arrived).astype(jnp.bfloat16)
    step_a = send(a_send, a_recv, twin)
    own_v[...] = dot(turned[:half], arrived)

    upstream = dot(gwin_v[...], arrived).astype(jnp.bfloat16)
    up_v[...] = upstream
    l_wout.wait()
    grad_att = dot(upstream, wout_v[...], NT)
    for w in range(2):
        for g in range(2):
            ga_v[w * 2 + g] = grad_att[w * WIN:(w + 1) * WIN, g * GROUP:(g + 1) * GROUP].astype(jnp.bfloat16)

    def backward(n, carry):
        spread(ga_v[n].astype(jnp.float32), gb_v, n, 1.0)
        grad_w = dot(qkv_v[2, n], gb_v[n], NT)
        weights = w_v[n]
        inner = jnp.sum(grad_w * weights, 0, keepdims=True)
        grad_s = (weights * (grad_w - inner)).astype(jnp.bfloat16)
        gp_v[0, n] = (gather(dot(grad_s, qkv_v[1, n], TN)) * 0.125).astype(jnp.bfloat16)
        gp_v[1, n] = dot(grad_s, qb_v[n]).astype(jnp.bfloat16)
        gp_v[2, n] = dot(wl_v[n], gb_v[n]).astype(jnp.bfloat16)
        return carry

    lax.fori_loop(0, 1, backward, 0, unroll=True)

    step_a.wait_recv()
    chunk = half // nx
    summed = own_v[...] + a_recv[...].astype(jnp.float32)
    own_v[...] = summed
    b_send[...] = summed.astype(jnp.bfloat16)
    step_b = [
        send(b_send.at[pl.ds(k * chunk, chunk)], b_recv.at[pl.ds((k - 1) * chunk, chunk)], on_x(k))
        for k in sorted(range(1, nx), key=lambda k: -min(k, nx - k))
    ]

    lax.fori_loop(1, 4, backward, 0, unroll=True)

    grad_proj = jnp.concatenate(
        [
            jnp.concatenate([gp_v[part, 2 * w + g] for part in range(3) for g in range(2)], 1)
            for w in range(2)
        ],
        0,
    )
    scaled = dot(grad_proj, wqkv_v[...], NT) * gain
    centred = cen_v[...]
    first = jnp.mean(scaled, -1, keepdims=True)
    second = jnp.mean(scaled * centred, -1, keepdims=True)
    branch = inv_v[:, 0:1] * (scaled - first - centred * second)
    result = (up_v[...].astype(jnp.float32) + branch).astype(jnp.bfloat16)
    back = dot(back_v[...], result).astype(jnp.bfloat16)
    ret_send[...] = back
    ret_recv[0:112, :] = back[0:112]
    ret_in = [
        send(block(ret_send, PART_AT[g], SIZE[g]), block(ret_recv, PART_AT[g], SIZE[g]), device)
        for g, device in (("10", near(0, 0, 1)), ("11", near(0, 1, 1)), ("01", near(0, 1, 0)))
    ]

    for copy in step_b:
        copy.wait_recv()
    total = own_v[0:chunk, :]
    for k in range(1, nx):
        total = total + b_recv[(k - 1) * chunk:k * chunk, :].astype(jnp.float32)
    own_v[0:chunk, :] = total
    low = total.astype(jnp.bfloat16)
    stacked = jnp.concatenate([low[:, q * 128:(q + 1) * 128] for q in range(4)], 0)
    c_send[...] = dot(regroup_v[...], stacked).astype(jnp.bfloat16)
    size = 4 * per

    @pl.when(z == 0)
    def _():
        pl.semaphore_wait(across_sem, ny)

    step_c = [
        send(block(c_send, k * size, size), block(c_recv, k * size, size), on_yz(k))
        for k in sorted(range(1, pieces), key=lambda k: -min(k // nz, ny - k // nz) - 4 * (k % nz))
    ]

    for copy in ret_in:
        copy.wait_recv()
    out_ref[...] = dot(home_v[...], ret_recv[...]).astype(jnp.bfloat16)
    for copy in step_c:
        copy.wait_recv()
    got = c_recv[size:2 * size].astype(jnp.float32)
    for k in range(2, pieces):
        got = got + c_recv[k * size:(k + 1) * size].astype(jnp.float32)
    wo_ref[...] = own_v[0:per, :] + jnp.concatenate([got[q * per:(q + 1) * per] for q in range(4)], 1)

    for copy in planned:
        copy.wait_send()


def on_device(sizes, acts, section_grads, gain, w_qkv, w_out, labels):
    pipe_n, nx, ny, nz = sizes
    per = D // (2 * nx * ny * nz)
    half = D // 2
    chunk = half // nx
    bf, f32 = jnp.bfloat16, jnp.float32
    table = layouts()
    sends = 3 + 4 + 3 + 1 + (nx - 1) + (ny * nz - 1)
    vm = pltpu.VMEM
    scratch = [
        vm((ACTS_ROWS, D), bf), vm((TOKENS, D), bf), vm((1, D), f32), vm((D, 3 * D), bf), vm((D, D), bf),
        vm(labels.shape, jnp.int32),
    ]
    scratch += [
        vm(table.shape, jnp.int32), vm((PART_ROWS, TOKENS), bf), vm((TOKENS, ACTS_ROWS), bf), vm((TOKENS, PART_ROWS), bf),
        vm((PART_ROWS, TOKENS), bf), vm((TOKENS, PART_ROWS), bf), vm((4 * chunk, 4 * chunk), bf),
    ]
    scratch += [
        vm((PART_ROWS - 112, D), bf), vm((PART_ROWS, D), bf), vm((PART_ROWS, D), bf), vm((PART_ROWS, D), bf), vm((PART_ROWS, D), bf),
    ]
    scratch += [
        vm((2, WIN, COLS), f32), vm((D, D), bf), vm((3, 4, WIN, GROUP), bf), vm((4, COLS, GROUP), bf),
        vm((4, WIN, COLS), f32), vm((4, WIN, COLS), bf), vm((4, WIN, GROUP), bf), vm((TOKENS, D), bf),
        vm((4, WIN, GROUP), bf), vm((4, COLS, GROUP), bf), vm((3, 4, WIN, GROUP), bf),
        vm((TOKENS, D), f32), vm((TOKENS, 128), f32),
    ]
    scratch += [
        vm((half, D), f32), vm((half, D), bf), vm((half, D), bf), vm((half, D), bf),
        vm((max(nx - 1, 1) * chunk, D), bf), vm((4 * chunk, 128), bf), vm((4 * chunk, 128), bf),
        pltpu.SemaphoreType.DMA((7,)),
        pltpu.SemaphoreType.DMA((sends,)), pltpu.SemaphoreType.DMA((sends,)), pltpu.SemaphoreType.REGULAR,
        pltpu.SemaphoreType.REGULAR,
    ]
    anywhere = pl.BlockSpec(memory_space=pltpu.HBM)
    out, wo = pl.pallas_call(
        functools.partial(kernel, sizes),
        out_shape=(pltpu.VMEM((TOKENS, D), bf), pltpu.VMEM((per, D), f32)),
        in_specs=[anywhere] * 7,
        out_specs=(pl.BlockSpec(memory_space=pltpu.VMEM), pl.BlockSpec(memory_space=pltpu.VMEM)),
        scratch_shapes=scratch,
        compiler_params=pltpu.CompilerParams(
            collective_id=0, has_side_effects=True, vmem_limit_bytes=60 * 1024 * 1024
        ),
        name="sublayer",
    )(
        acts.reshape(TOKENS, D), section_grads.reshape(TOKENS, D), gain, w_qkv[0], w_out[0], labels,
        jnp.asarray(table),
    )
    return out.reshape(acts.shape), wo


def solution(mesh):
    pipe_n, lon_n, lat_n = (mesh.shape[axis] for axis in ("pipe", "lon", "lat"))
    ny = 8 if lon_n == 32 else min(lon_n, 2)
    sizes = (pipe_n, lon_n // ny, ny, lat_n // 2)
    in_specs = (
        P("pipe", None, "lat", "lon", None),
        P("pipe", None, "lat", "lon", None),
        P("pipe", None),
        P("pipe", None, None),
        P("pipe", None, None),
        P(),
    )
    out_specs = (P("pipe", None, "lat", "lon", None), P(("pipe", "lon", "lat"), None))
    return jax.shard_map(
        functools.partial(on_device, sizes), mesh=mesh, in_specs=in_specs, out_specs=out_specs, check_vma=False
    )
```

```python
import functools

import jax
import jax.numpy as jnp
import numpy as np
from jax import lax
from jax.experimental import pallas as pl
from jax.experimental.pallas import tpu as pltpu
from jax.sharding import PartitionSpec as P

MESH = pl.DeviceIdType.MESH
LEV = 2
LAT_CELLS = 6
LON_CELLS = 24
TOKENS = 288
WIN = 144
D = 512
GROUP = 256
HEADS = 4
COLS = HEADS * WIN
PART_AT = {"00": 0, "10": 112, "01": 224, "11": 272}
PART_ROWS = 320
ACTS_AT = {"own": 0, "10": 288, "01": 400, "11": 448}
ACTS_ROWS = 496
SIZE = {"00": 112, "10": 112, "01": 48, "11": 48}
epsilon = 1e-05
masked_score = -1e30
open_score = 3e38


def natural(lev, row, col):
    return (lev * LAT_CELLS + row) * LON_CELLS + col


def cells(group, part):
    rows = range(0, 3) if group[0] == "1" else range(3, 6)
    if group[1] == "1":
        cols = range(0, 6) if part == 1 else ()
    else:
        cols = range(6, 18) if part == 0 else range(18, 24)
    return [(l, r, c) for l in range(LEV) for r in rows for c in cols]


def layouts():
    groups = ("00", "10", "01", "11")
    place = {g: {cell: n for n, cell in enumerate(cells(g, 0) + cells(g, 1))} for g in groups}

    table = np.full((PART_ROWS, 8), -1, np.int32)
    order = [(g, cell) for w in range(2) for g in groups for cell in cells(g, w)]
    for t, (g, cell) in enumerate(order):
        n = place[g][cell]
        table[PART_AT[g] + n, 0] = natural(*cell)
        table[PART_AT[g] + n, 1] = t
        table[t, 2] = natural(*cell) if g == "00" else ACTS_AT[g] + n
        table[t, 3] = PART_AT[g] + n
        table[natural(*cell), 4] = PART_AT[g] + n
        table[t, 5] = cell[1] + (6 if g[0] == "1" else 0)
        table[t, 6] = cell[2] + (24 if g[1] == "1" else 0)
    return table


def dot(left, right, dims=((1,), (0,))):
    return lax.dot_general(left, right, (dims, ((), ())), preferred_element_type=jnp.float32)


NT = ((1,), (1,))
TN = ((0,), (0,))


def kernel(
    sizes,
    acts_hbm, grads_hbm, gain_hbm, wqkv_hbm, wout_hbm, labels_hbm,
    table_hbm,
    out_ref, wo_ref,
    acts_buf, grads_v, gain_v, wqkv_v, wout_v, labels_v,
    table_v,
    part_v, awin_v, gwin_v, back_v, home_v, regroup_v,
    acts_part, grads_part, grads_buf, ret_send, ret_recv,
    mask_v, perm_v, qkv_v, qb_v, w_v, wl_v, att_v, up_v, ga_v, gb_v, gp_v, cen_v, inv_v,
    own_v, a_send, a_recv, b_send, b_recv, c_send, c_recv,
    in_sem, send_sem, recv_sem, ready_sem, across_sem,
):
    pipe_n, nx, ny, nz = sizes
    lon_n, lat_n = nx * ny, nz * 2
    s = lax.axis_index("pipe")
    j = lax.axis_index("lon")
    i = lax.axis_index("lat")
    x, y = j // ny, j % ny
    z, core = i // 2, i % 2

    def near(ds, dj, di):
        return (
            (s + ds + pipe_n) % pipe_n if ds else s,
            (j + dj + lon_n) % lon_n if dj else j,
            (i + di + lat_n) % lat_n if di else i,
        )

    def on_x(k):
        return (s, ((x + k) % nx) * ny + y, i)

    def on_yz(k):
        return (s, x * ny + (y + k // nz) % ny, (z + k % nz) % nz * 2 + core)

    twin = (s, j, z * 2 + (1 - core))

    loads = []
    for n, (src, dst) in enumerate((
        (table_hbm, table_v), (acts_hbm, acts_buf.at[pl.ds(0, TOKENS)]), (grads_hbm, grads_v), (labels_hbm, labels_v),
        (gain_hbm, gain_v), (wqkv_hbm, wqkv_v), (wout_hbm, wout_v),
    )):
        load = pltpu.make_async_copy(src, dst, in_sem.at[n])
        load.start()
        loads.append(load)
    l_table, l_acts, l_grads, l_labels, l_gain, l_wqkv, l_wout = loads

    barrier = pltpu.get_barrier_semaphore()
    greeted = [near(0, 0, 1), near(0, 1, 1), near(0, 0, -1), near(0, -1, -1), near(0, 1, 0), near(0, -1, 0), twin]
    greeted += [on_x(k) for k in range(1, nx)] + [on_yz(k * nz) for k in range(1, ny)]
    across = [on_yz(k * nz + 1) for k in range(ny)]
    before = [near(-1, 0, 0), near(-1, 0, -1), near(-1, -1, 0), near(-1, -1, -1)]
    after = [near(1, 0, 0), near(1, 0, 1), near(1, 1, 0), near(1, 1, 1)]
    last = pipe_n - 1

    def greet(devices):
        for device in devices:
            pl.semaphore_signal(barrier, inc=1, device_id=device, device_id_type=MESH)

    greet(greeted)

    @pl.when(s != last)
    def _():
        greet(after)

    @pl.when(s == 0)
    def _():
        greet(before)

    @pl.when(z == 0)
    def _():
        greet(across)


    def picks(column, rows, cols):
        found = table_v[0:rows, column:column + 1] == lax.broadcasted_iota(jnp.int32, (rows, cols), 1)
        return found.astype(jnp.float32)

    planned = []

    def plan(src, dst, device):
        n = len(planned)
        copy = pltpu.make_async_remote_copy(
            src_ref=src, dst_ref=dst, send_sem=send_sem.at[n], recv_sem=recv_sem.at[n],
            device_id=device, device_id_type=MESH,
        )
        planned.append(copy)
        return copy

    def send(src, dst, device):
        copy = plan(src, dst, device)
        copy.start()
        return copy

    def block(ref, at, size):
        return ref.at[pl.ds(at, size)]

    here = {"10": (0, -1), "11": (-1, -1), "00": (0, 0), "01": (-1, 0)}
    acts_in = [
        plan(block(acts_part, PART_AT[g] - 112, SIZE[g]), block(acts_buf, ACTS_AT[g], SIZE[g]), near(0, *here[g]))
        for g in ("10", "11", "01")
    ]
    grads_in = [
        plan(block(grads_part, PART_AT[g], SIZE[g]), block(grads_buf, PART_AT[g], SIZE[g]), near(-1, *here[g]))
        for g in ("10", "11", "00", "01")
    ]

    l_table.wait()
    part_v[...] = picks(0, PART_ROWS, TOKENS).astype(jnp.bfloat16)
    l_acts.wait()
    acts_part[...] = dot(part_v[112:], acts_buf[0:TOKENS]).astype(jnp.bfloat16)
    l_grads.wait()
    grads_part[...] = dot(part_v[...], grads_v[...]).astype(jnp.bfloat16)
    pl.semaphore_wait(barrier, len(greeted) + jnp.where(s > 0, 4, 0) + jnp.where(s == last, 4, 0) + jnp.where(z > 0, ny, 0))

    @pl.when(s == last)
    def _():
        for device in after:
            pl.semaphore_signal(ready_sem, inc=1, device_id=device, device_id_type=MESH)

    @pl.when(z > 0)
    def _():
        for device in across:
            pl.semaphore_signal(across_sem, inc=1, device_id=device, device_id_type=MESH)

    for copy in acts_in:
        copy.start()

    @pl.when(s != 0)
    def _():
        for copy in grads_in:
            copy.start()

    l_labels.wait()
    row_n, col_n = labels_v.shape
    cell = lax.broadcasted_iota(jnp.int32, (col_n, 128), 0) - j * LON_CELLS
    cell = jnp.where(cell < 0, cell + col_n, cell)
    pick_col = (cell == lax.broadcasted_iota(jnp.int32, (col_n, 128), 1)).astype(jnp.float32)
    row = lax.broadcasted_iota(jnp.int32, (row_n, row_n), 1) - i * LAT_CELLS
    row = jnp.where(row < 0, row + row_n, row)
    pick_row = (row == lax.broadcasted_iota(jnp.int32, (row_n, row_n), 0)).astype(jnp.float32)
    near_labels = dot(pick_row, dot(labels_v[...].astype(jnp.float32), pick_col))
    token_label = jnp.sum(dot(picks(5, TOKENS, row_n), near_labels) * picks(6, TOKENS, 128), -1, keepdims=True)
    lane = lax.broadcasted_iota(jnp.int32, (TOKENS, 128), 1).astype(jnp.float32)
    one_hot = (token_label == lane).astype(jnp.float32).astype(jnp.bfloat16)
    for w in range(2):
        here = one_hot[w * WIN:(w + 1) * WIN]
        alike = dot(here, jnp.concatenate([here] * HEADS, 0), NT)
        mask_v[w] = jnp.where(alike > 0.5, open_score, masked_score)

    per = D // (2 * nx * ny * nz)
    m = lax.broadcasted_iota(jnp.int32, (D, D), 0)
    r_at = m % per
    z_at = (m // per) % nz
    y_at = (m // (per * nz)) % ny
    x_at = (m // (per * nz * ny)) % nx
    c_at = m // (per * nz * ny * nx)
    feature = (
        (((x_at + x) % nx * ny + (y_at + y) % ny) * nz + (z_at + z) % nz) * 2 + (c_at + core) % 2
    ) * per + r_at
    perm_v[...] = (feature == lax.broadcasted_iota(jnp.int32, (D, D), 1)).astype(jnp.float32).astype(jnp.bfloat16)

    awin_v[...] = picks(2, TOKENS, ACTS_ROWS).astype(jnp.bfloat16)
    gwin_v[...] = picks(3, TOKENS, PART_ROWS).astype(jnp.bfloat16)
    back_v[...] = picks(1, PART_ROWS, TOKENS).astype(jnp.bfloat16)
    home_v[...] = picks(4, TOKENS, PART_ROWS).astype(jnp.bfloat16)
    pieces = ny * nz
    m = lax.broadcasted_iota(jnp.int32, regroup_v.shape, 0)
    old = (m // per) % 4 * (pieces * per) + m // (4 * per) * per + m % per
    regroup_v[...] = (old == lax.broadcasted_iota(jnp.int32, regroup_v.shape, 1)).astype(jnp.float32).astype(jnp.bfloat16)

    l_gain.wait()
    l_wqkv.wait()
    for copy in acts_in:
        copy.wait_recv()
    gain = gain_v[...]
    inputs = dot(awin_v[...], acts_buf[...])
    mean = jnp.mean(inputs, -1, keepdims=True)
    centred = inputs - mean
    inverse = 1.0 / jnp.sqrt(jnp.mean(centred * centred, -1, keepdims=True) + epsilon)
    centred = centred * inverse
    cen_v[...] = centred
    inv_v[...] = jnp.broadcast_to(inverse, inv_v.shape)
    projected = dot((centred * gain).astype(jnp.bfloat16), wqkv_v[...])
    for part in range(3):
        for w in range(2):
            for g in range(2):
                at = part * D + g * GROUP
                qkv_v[part, w * 2 + g] = projected[w * WIN:(w + 1) * WIN, at:at + GROUP].astype(jnp.bfloat16)

    head_lane = lax.broadcasted_iota(jnp.int32, (1, GROUP), 1) // 64
    head_mask = [(head_lane == h).astype(jnp.float32) for h in range(HEADS)]

    def spread(block, dst, n, scale):
        for h in range(HEADS):
            dst[n, h * WIN:(h + 1) * WIN, :] = block * (head_mask[h] * scale).astype(jnp.bfloat16)

    def gather(product):
        total = product[0:WIN] * head_mask[0]
        for h in range(1, HEADS):
            total = total + product[h * WIN:(h + 1) * WIN] * head_mask[h]
        return total

    def forward(n, carry):
        spread(qkv_v[0, n], qb_v, n, 0.125)
        scores = jnp.minimum(dot(qkv_v[1, n], qb_v[n], NT), mask_v[n // 2])
        exps = jnp.exp(scores - jnp.max(scores, 0, keepdims=True))
        weights = exps * (1.0 / jnp.sum(exps, 0, keepdims=True))
        w_v[n] = weights
        low = weights.astype(jnp.bfloat16)
        wl_v[n] = low
        att_v[n] = gather(dot(low, qkv_v[2, n], TN)).astype(jnp.bfloat16)
        return carry

    @pl.when(s == 0)
    def _():
        pl.semaphore_wait(ready_sem, 4)
        for copy in grads_in:
            copy.start()

    lax.fori_loop(0, 4, forward, 0, unroll=True)

    attended = jnp.concatenate(
        [jnp.concatenate([att_v[2 * w], att_v[2 * w + 1]], 1) for w in range(2)], 0
    )
    attended = dot(back_v[...], attended).astype(jnp.bfloat16)
    turned = dot(perm_v[...], attended, NT).astype(jnp.bfloat16)
    half = D // 2
    for copy in grads_in:
        copy.wait_recv()
    arrived = grads_buf[...]
    quarter = half // 2
    step_a = []
    for at in (0, quarter):
        a_send[at:at + quarter, :] = dot(turned[half + at:half + at + quarter], arrived).astype(jnp.bfloat16)
        step_a.append(send(block(a_send, at, quarter), block(a_recv, at, quarter), twin))
    own_v[...] = dot(turned[:half], arrived)

    upstream = dot(gwin_v[...], arrived).astype(jnp.bfloat16)
    up_v[...] = upstream
    l_wout.wait()
    grad_att = dot(upstream, wout_v[...], NT)
    for w in range(2):
        for g in range(2):
            ga_v[w * 2 + g] = grad_att[w * WIN:(w + 1) * WIN, g * GROUP:(g + 1) * GROUP].astype(jnp.bfloat16)

    def backward(n, carry):
        spread(ga_v[n], gb_v, n, 1.0)
        grad_w = dot(qkv_v[2, n], gb_v[n], NT)
        weights = w_v[n]
        inner = jnp.sum(grad_w * weights, 0, keepdims=True)
        grad_s = (weights * (grad_w - inner)).astype(jnp.bfloat16)
        gp_v[0, n] = (gather(dot(grad_s, qkv_v[1, n], TN)) * 0.125).astype(jnp.bfloat16)
        gp_v[1, n] = dot(grad_s, qb_v[n]).astype(jnp.bfloat16)
        gp_v[2, n] = dot(wl_v[n], gb_v[n]).astype(jnp.bfloat16)
        return carry

    lax.fori_loop(0, 1, backward, 0, unroll=True)

    for copy in step_a:
        copy.wait_recv()
    chunk = half // nx
    step_b = []
    for k in sorted(range(nx), key=lambda k: (k == 0, -min(k, nx - k))):
        rows = slice(k * chunk, (k + 1) * chunk)
        summed = own_v[rows, :] + a_recv[rows, :].astype(jnp.float32)
        if k == 0:
            own_v[rows, :] = summed
        else:
            b_send[rows, :] = summed.astype(jnp.bfloat16)
            step_b.append(send(block(b_send, k * chunk, chunk), block(b_recv, (k - 1) * chunk, chunk), on_x(k)))

    lax.fori_loop(1, 4, backward, 0, unroll=True)

    grad_proj = jnp.concatenate(
        [
            jnp.concatenate([gp_v[part, 2 * w + g] for part in range(3) for g in range(2)], 1)
            for w in range(2)
        ],
        0,
    )
    scaled = dot(grad_proj, wqkv_v[...], NT) * gain
    centred = cen_v[...]
    first = jnp.mean(scaled, -1, keepdims=True)
    second = jnp.mean(scaled * centred, -1, keepdims=True)
    branch = inv_v[:, 0:1] * (scaled - first - centred * second)
    result = (up_v[...].astype(jnp.float32) + branch).astype(jnp.bfloat16)
    ret_in = []
    for g, device in (("10", near(0, 0, 1)), ("11", near(0, 1, 1)), ("01", near(0, 1, 0))):
        rows = slice(PART_AT[g], PART_AT[g] + SIZE[g])
        ret_send[rows, :] = dot(back_v[rows, :], result).astype(jnp.bfloat16)
        ret_in.append(send(block(ret_send, PART_AT[g], SIZE[g]), block(ret_recv, PART_AT[g], SIZE[g]), device))
    ret_recv[0:112, :] = dot(back_v[0:112, :], result).astype(jnp.bfloat16)

    for copy in step_b:
        copy.wait_recv()
    total = own_v[0:chunk, :]
    for k in range(1, nx):
        total = total + b_recv[(k - 1) * chunk:k * chunk, :].astype(jnp.float32)
    own_v[0:chunk, :] = total
    low = total.astype(jnp.bfloat16)
    stacked = jnp.concatenate([low[:, q * 128:(q + 1) * 128] for q in range(4)], 0)
    c_send[...] = dot(regroup_v[...], stacked).astype(jnp.bfloat16)
    size = 4 * per

    @pl.when(z == 0)
    def _():
        pl.semaphore_wait(across_sem, ny)

    step_c = [
        send(block(c_send, k * size, size), block(c_recv, k * size, size), on_yz(k))
        for k in sorted(range(1, pieces), key=lambda k: -min(k // nz, ny - k // nz) - 4 * (k % nz))
    ]

    for copy in ret_in:
        copy.wait_recv()
    out_ref[...] = dot(home_v[...], ret_recv[...]).astype(jnp.bfloat16)
    for copy in step_c:
        copy.wait_recv()
    got = c_recv[size:2 * size].astype(jnp.float32)
    for k in range(2, pieces):
        got = got + c_recv[k * size:(k + 1) * size].astype(jnp.float32)
    wo_ref[...] = own_v[0:per, :] + jnp.concatenate([got[q * per:(q + 1) * per] for q in range(4)], 1)

    for copy in planned:
        copy.wait_send()


def on_device(sizes, acts, section_grads, gain, w_qkv, w_out, labels):
    pipe_n, nx, ny, nz = sizes
    per = D // (2 * nx * ny * nz)
    half = D // 2
    chunk = half // nx
    bf, f32 = jnp.bfloat16, jnp.float32
    table = layouts()
    sends = 3 + 4 + 3 + 2 + (nx - 1) + (ny * nz - 1)
    vm = pltpu.VMEM
    scratch = [
        vm((ACTS_ROWS, D), bf), vm((TOKENS, D), bf), vm((1, D), f32), vm((D, 3 * D), bf), vm((D, D), bf),
        vm(labels.shape, jnp.int32),
    ]
    scratch += [
        vm(table.shape, jnp.int32), vm((PART_ROWS, TOKENS), bf), vm((TOKENS, ACTS_ROWS), bf), vm((TOKENS, PART_ROWS), bf),
        vm((PART_ROWS, TOKENS), bf), vm((TOKENS, PART_ROWS), bf), vm((4 * chunk, 4 * chunk), bf),
    ]
    scratch += [
        vm((PART_ROWS - 112, D), bf), vm((PART_ROWS, D), bf), vm((PART_ROWS, D), bf), vm((PART_ROWS, D), bf), vm((PART_ROWS, D), bf),
    ]
    scratch += [
        vm((2, WIN, COLS), f32), vm((D, D), bf), vm((3, 4, WIN, GROUP), bf), vm((4, COLS, GROUP), bf),
        vm((4, WIN, COLS), f32), vm((4, WIN, COLS), bf), vm((4, WIN, GROUP), bf), vm((TOKENS, D), bf),
        vm((4, WIN, GROUP), bf), vm((4, COLS, GROUP), bf), vm((3, 4, WIN, GROUP), bf),
        vm((TOKENS, D), f32), vm((TOKENS, 128), f32),
    ]
    scratch += [
        vm((half, D), f32), vm((half, D), bf), vm((half, D), bf), vm((half, D), bf),
        vm((max(nx - 1, 1) * chunk, D), bf), vm((4 * chunk, 128), bf), vm((4 * chunk, 128), bf),
        pltpu.SemaphoreType.DMA((7,)),
        pltpu.SemaphoreType.DMA((sends,)), pltpu.SemaphoreType.DMA((sends,)), pltpu.SemaphoreType.REGULAR,
        pltpu.SemaphoreType.REGULAR,
    ]
    anywhere = pl.BlockSpec(memory_space=pltpu.HBM)
    out, wo = pl.pallas_call(
        functools.partial(kernel, sizes),
        out_shape=(pltpu.VMEM((TOKENS, D), bf), pltpu.VMEM((per, D), f32)),
        in_specs=[anywhere] * 7,
        out_specs=(pl.BlockSpec(memory_space=pltpu.VMEM), pl.BlockSpec(memory_space=pltpu.VMEM)),
        scratch_shapes=scratch,
        compiler_params=pltpu.CompilerParams(
            collective_id=0, has_side_effects=True, vmem_limit_bytes=60 * 1024 * 1024
        ),
        name="sublayer",
    )(
        acts.reshape(TOKENS, D), section_grads.reshape(TOKENS, D), gain, w_qkv[0], w_out[0], labels,
        jnp.asarray(table),
    )
    return out.reshape(acts.shape), wo


def solution(mesh):
    pipe_n, lon_n, lat_n = (mesh.shape[axis] for axis in ("pipe", "lon", "lat"))
    ny = 8 if lon_n == 32 else min(lon_n, 2)
    sizes = (pipe_n, lon_n // ny, ny, lat_n // 2)
    in_specs = (
        P("pipe", None, "lat", "lon", None),
        P("pipe", None, "lat", "lon", None),
        P("pipe", None),
        P("pipe", None, None),
        P("pipe", None, None),
        P(),
    )
    out_specs = (P("pipe", None, "lat", "lon", None), P(("pipe", "lon", "lat"), None))
    return jax.shard_map(
        functools.partial(on_device, sizes), mesh=mesh, in_specs=in_specs, out_specs=out_specs, check_vma=False
    )
```
